256 devices in a mesh: grid: 16 (over z_hi, y, core), mesh: 16 (over z_lo, x).
Axes of the slice: x: 4, y: 4, z: 8 (z_hi: 2, z_lo: 4; z = z_hi * 4 + z_lo), core: 2. Of those that a mesh axis runs over, the one named last changes fastest.
Arguments:
- grid_latent: bfloat16 [65536, 512], P(('grid', 'mesh')), may hold values from -6 to 6
- mesh_latent: bfloat16 [32768, 512], P(('grid', 'mesh')), may hold values from -6 to 6
- mesh_cotangent: bfloat16 [32768, 512], P(('grid', 'mesh')), may hold values from -6 to 6
- weights: bfloat16 [12, 512, 512], replicated, may hold values from -0.25 to 0.25
- biases: float32 [4, 512], replicated, may hold values from -3 to 3
- norm_gains: float32 [4, 512], replicated, may hold values from 0.25 to 1.75
- grid_send_rows: int32 [256, 16, 16], P(('grid', 'mesh')), may hold values from 0 to 255
- grid_edge_counts: int32 [256, 16], P(('grid', 'mesh')), may hold values from 1 to 16, as said below
- grid_edge_targets: int32 [256, 3, 16, 16], P(('grid', 'mesh')), may hold values from -1 to 127, as said below
- mesh_senders: int32 [256, 512], P(('grid', 'mesh')), may hold values from 0 to 383
- mesh_receivers: int32 [256, 512], P(('grid', 'mesh')), may hold values from 0 to 127
- halo_rows: int32 [256, 16, 16], P(('grid', 'mesh')), may hold values from 0 to 127
Outputs:
- mesh_out: bfloat16 [32768, 512], P(('grid', 'mesh'))
- grid_grad: float32 [65536, 512], P(('grid', 'mesh'))
- mesh_grad: float32 [32768, 512], P(('grid', 'mesh'))
- weight_grad: float32 [4, 787456], P(None, ('grid', 'mesh'))
The draws below stay inside these ranges and needn't reach their ends.
Inputs may be any that keep to these rules, and one draw needn't show every extreme that they name: `grid_edge_counts`: at most 16 live slots come from one source block to one receiving block, and in every draw some receiving block gets 16 from each of its 16 sources; entries at or past the count carry no edge. `grid_edge_targets`: -1 marks an absent edge; edge position 0 of a slot is never absent.
All inputs are finite; a program needn't handle non-finite values.
Results may differ from the reference program's by a relative error of at most 0.023.
Values may be sent and summed in bfloat16 or wider, within the bound.
A program may use at most 128 MiB of HBM per device.

```python
import math
import jax
import jax.numpy as jnp
from jax import lax

D = 512
GRID_DEV = 256
MESH_DEV = 128
CAP = 16
FAN = 3
EDGE_DEV = 512
HALO = 16
SOURCES = 16
PEERS = 16
BLOCKS = 256
GRID_NODES = 65536
MESH_NODES = 32768
N_GRID = 16
N_MESH = 16


def draw_grid_edge_counts(key, part):
    key = jax.random.fold_in(key, 11)
    destination = jnp.arange(BLOCKS) // PEERS
    distance = jnp.abs(2 * destination - (SOURCES - 1))
    spread_base = max((SOURCES - 1) ** 2, 1)
    weight = 1 + 7 * distance * distance // spread_base
    highest = jnp.maximum(weight * CAP // 8, max(3 * CAP // 4, 1))
    drawn_bits = jax.random.randint(key, (BLOCKS, SOURCES), 0, 1 << 20)
    counts = 1 + drawn_bits % highest[:, None]
    chosen = jax.random.randint(jax.random.fold_in(key, 5), (), 0, BLOCKS)
    counts = jnp.where(jnp.arange(BLOCKS)[:, None] == chosen, CAP, counts)
    return counts.astype(jnp.int32)


def draw_grid_edge_targets(key, part):
    key = jax.random.fold_in(key, 23)
    target_key, keep_key = jax.random.split(key)
    dimensions = (BLOCKS, FAN, SOURCES, CAP)
    picked = jax.random.randint(target_key, dimensions, 0, MESH_DEV)
    kept = jax.random.randint(keep_key, dimensions, 0, 2)
    leading = (jnp.arange(FAN) == 0)[None, :, None, None]
    return jnp.where(leading | (kept == 1), picked, -1).astype(jnp.int32)


def with_ends(entries, stream_key, least, largest):
    spot = [jax.random.randint(jax.random.fold_in(stream_key, axis), (), 0, length) for axis, length in enumerate(entries.shape)]
    main_axis = entries.shape.index(max(entries.shape))
    next_to = spot[:main_axis] + [(spot[main_axis] + 1) % entries.shape[main_axis]] + spot[main_axis + 1:]
    return entries.at[tuple(spot)].set(least).at[tuple(next_to)].set(largest)


def shard_levels(rng, extent, shards, least, top_value):
    loudness, own = 1.0, jax.random.fold_in(rng, 6)
    for axis_at, blocks in shards:
        steps = jnp.exp(jax.random.uniform(jax.random.fold_in(own, axis_at), (blocks,), jnp.float32, least / len(shards), top_value / len(shards)))
        loudness = loudness * jnp.repeat(steps, extent[axis_at] // blocks).reshape([-1 if axis == axis_at else 1 for axis in range(len(extent))])
    return loudness


def noise(own_key, dims, spread, bound, cuts=(), dtype=jnp.bfloat16):
    factor_of = shard_levels(own_key, dims, cuts, -0.22, 0.18) if cuts else 1.0
    entries = jax.random.normal(own_key, dims, jnp.float32) * spread * factor_of
    return jnp.minimum(jnp.maximum(entries, -bound), bound).astype(dtype)


def setup_inputs(seed: int = 0) -> dict:
    keys = jax.random.split(jax.random.key(seed), 13)
    grid_latent = noise(keys[0], (GRID_NODES, D), 1.0, 6.0, ((0, 256),))
    mesh_latent = noise(keys[1], (MESH_NODES, D), 1.0, 6.0, ((0, 256),))
    mesh_cotangent = noise(keys[2], (MESH_NODES, D), 1.0, 6.0, ((0, 256),))
    weights = noise(keys[3], (12, D, D), D ** -0.5, 0.25)
    biases = noise(keys[4], (4, D), 0.5, 3.0, (), jnp.float32)
    norm_gains = jnp.clip(1.0 + 0.15 * jax.random.normal(keys[5], (4, D), jnp.float32), 0.25, 1.75)
    grid_send_rows = with_ends(jax.random.randint(keys[6], (BLOCKS, SOURCES, CAP), 0, GRID_DEV), jax.random.fold_in(keys[6], 1), 0, GRID_DEV - 1).astype(jnp.int32)
    grid_edge_counts = draw_grid_edge_counts(jax.random.fold_in(keys[12], 71), 0)
    grid_edge_targets = draw_grid_edge_targets(jax.random.fold_in(keys[12], 71), 0)
    mesh_senders = with_ends(jax.random.randint(keys[9], (BLOCKS, EDGE_DEV), 0, MESH_DEV + PEERS * HALO), jax.random.fold_in(keys[9], 1), 0, (MESH_DEV + PEERS * HALO) - 1).astype(jnp.int32)
    mesh_receivers = with_ends(jax.random.randint(keys[10], (BLOCKS, EDGE_DEV), 0, MESH_DEV), jax.random.fold_in(keys[10], 1), 0, MESH_DEV - 1).astype(jnp.int32)
    halo_rows = with_ends(jax.random.randint(keys[11], (BLOCKS, PEERS, HALO), 0, MESH_DEV), jax.random.fold_in(keys[11], 1), 0, MESH_DEV - 1).astype(jnp.int32)
    return dict(grid_latent=grid_latent, mesh_latent=mesh_latent, mesh_cotangent=mesh_cotangent, weights=weights, biases=biases, norm_gains=norm_gains, grid_send_rows=grid_send_rows, grid_edge_counts=grid_edge_counts, grid_edge_targets=grid_edge_targets, mesh_senders=mesh_senders, mesh_receivers=mesh_receivers, halo_rows=halo_rows)


epsilon = 1e-05

def project(left, weight):
    return jnp.dot(left, weight, preferred_element_type=jnp.float32)

def row_contract(left, right):
    return lax.dot_general(left, right, (((0,), (0,)), ((), ())), preferred_element_type=jnp.float32)

def through_weight(grad, weight):
    return lax.dot_general(grad, weight, (((1,), (1,)), ((), ())), preferred_element_type=jnp.float32)

def swish_slope(values):
    sigmoid_value = jax.nn.sigmoid(values)
    return sigmoid_value * (1.0 + values * (1.0 - sigmoid_value))

def perceptron(summed, offset, out_weight, scales):
    hidden = jax.nn.silu(summed + offset).astype(jnp.bfloat16)
    projected = project(hidden, out_weight)
    centered = projected - lax.optimization_barrier(jnp.mean(projected, axis=-1, keepdims=True))
    reciprocal = lax.rsqrt(lax.optimization_barrier(jnp.mean(centered * centered, axis=-1, keepdims=True)) + epsilon)
    normed = centered * reciprocal
    return (normed * scales, hidden, normed, reciprocal)

def perceptron_back(upstream, summed, offset, out_weight, scales, hidden, normed, reciprocal):
    scale_grad = lax.optimization_barrier(jnp.sum(upstream * normed, axis=0))
    weighted = upstream * scales
    inner_grad = reciprocal * (weighted - lax.optimization_barrier(jnp.mean(weighted, axis=-1, keepdims=True)) - normed * lax.optimization_barrier(jnp.mean(weighted * normed, axis=-1, keepdims=True)))
    inner_half = inner_grad.astype(jnp.bfloat16)
    matrix_grad = row_contract(hidden, inner_half)
    hidden_grad = through_weight(inner_half, out_weight)
    summed_grad = hidden_grad * swish_slope(summed + offset)
    offset_grad = lax.optimization_barrier(jnp.sum(summed_grad, axis=0))
    return (summed_grad.astype(jnp.bfloat16), matrix_grad, offset_grad, scale_grad)

def pack_bucket(first, second, third, offset_grad, scale_grad):
    return jnp.concatenate([first.reshape(-1), second.reshape(-1), third.reshape(-1), offset_grad, scale_grad])

def reference(grid_latent, mesh_latent, mesh_cotangent, weights, biases, norm_gains, grid_send_rows, grid_edge_counts, grid_edge_targets, mesh_senders, mesh_receivers, halo_rows):
    blocks = N_GRID * N_MESH
    sender_all = project(grid_latent, weights[0]).astype(jnp.bfloat16).reshape(blocks, GRID_DEV, D)
    lower_rows = mesh_latent.reshape(blocks, MESH_DEV, D)
    cotangent = mesh_cotangent.reshape(blocks, MESH_DEV, D)
    slot_range = jnp.arange(CAP)
    halo_range = jnp.arange(HALO)

    def encoder_parts(block_id):
        grid_index = block_id // N_MESH
        mesh_index = block_id % N_MESH
        sources = jnp.arange(N_GRID) * N_MESH + mesh_index
        slot_rows = grid_send_rows[sources, grid_index]
        slot_terms = sender_all[sources[:, None], slot_rows].reshape(N_GRID * CAP, D).astype(jnp.float32)
        live_slots = slot_range[None, :] < grid_edge_counts[block_id][:, None]
        targets = grid_edge_targets[block_id]
        present = (live_slots[None] & (targets >= 0)).reshape(-1, 1).astype(jnp.float32)
        target_index = jnp.where(targets >= 0, targets, 0).reshape(-1)
        node_rows = lower_rows[block_id]
        grid_summed = jnp.tile(slot_terms, (FAN, 1)) + project(node_rows, weights[1])[target_index]
        grid_out, grid_hidden, grid_normed, grid_inverse = perceptron(grid_summed, biases[0], weights[2], norm_gains[0])
        grid_gathered = jax.ops.segment_sum(grid_out * present, target_index, num_segments=MESH_DEV).astype(jnp.bfloat16)
        low_summed = project(node_rows, weights[3]) + project(grid_gathered, weights[4])
        low_out, low_hidden, low_normed, low_inverse = perceptron(low_summed, biases[1], weights[5], norm_gains[1])
        middle = (node_rows.astype(jnp.float32) + low_out).astype(jnp.bfloat16)
        return (present, target_index, node_rows, grid_summed, grid_hidden, grid_normed, grid_inverse, grid_gathered, low_summed, low_hidden, low_normed, low_inverse, middle)

    def encoder_middle(block_id):
        return encoder_parts(block_id)[-1]
    middle_all = lax.map(encoder_middle, jnp.arange(blocks))
    table_all = project(middle_all.reshape(-1, D), weights[6]).astype(jnp.bfloat16).reshape(blocks, MESH_DEV, D)

    def processor_step(totals, block_id):
        grid_index = block_id // N_MESH
        mesh_index = block_id % N_MESH
        peer_ids = grid_index * N_MESH + jnp.arange(N_MESH)
        halo_terms = table_all[peer_ids[:, None], halo_rows[peer_ids, mesh_index]]
        sender_table = jnp.concatenate([table_all[block_id], halo_terms.reshape(-1, D)], axis=0)
        middle = middle_all[block_id]
        senders = mesh_senders[block_id]
        receivers = mesh_receivers[block_id]
        mesh_summed = sender_table[senders].astype(jnp.float32) + project(middle, weights[7])[receivers]
        edge_out, mesh_hidden, mesh_normed, mesh_inverse = perceptron(mesh_summed, biases[2], weights[8], norm_gains[2])
        mesh_gathered = jax.ops.segment_sum(edge_out, receivers, num_segments=MESH_DEV).astype(jnp.bfloat16)
        top_summed = project(middle, weights[9]) + project(mesh_gathered, weights[10])
        top_out, top_hidden, top_normed, top_inverse = perceptron(top_summed, biases[3], weights[11], norm_gains[3])
        upper_rows = (middle.astype(jnp.float32) + top_out).astype(jnp.bfloat16)
        upstream = cotangent[block_id].astype(jnp.float32)
        top_grad, top_weight_grad, top_offset_grad, top_scale_grad = perceptron_back(upstream, top_summed, biases[3], weights[11], norm_gains[3], top_hidden, top_normed, top_inverse)
        middle_grad = upstream + through_weight(top_grad, weights[9])
        gathered_grad = through_weight(top_grad, weights[10])
        edge_grad, edge_weight_grad, edge_offset_grad, edge_scale_grad = perceptron_back(gathered_grad[receivers], mesh_summed, biases[2], weights[8], norm_gains[2], mesh_hidden, mesh_normed, mesh_inverse)
        edge_float = edge_grad.astype(jnp.float32)
        receiver_half = jax.ops.segment_sum(edge_float, receivers, num_segments=MESH_DEV).astype(jnp.bfloat16)
        table_grad = jax.ops.segment_sum(edge_float, senders, num_segments=MESH_DEV + N_MESH * HALO)
        middle_grad = middle_grad + through_weight(receiver_half, weights[7])
        terms = (row_contract(middle, receiver_half), edge_weight_grad, row_contract(middle, top_grad), row_contract(mesh_gathered, top_grad), top_weight_grad, edge_offset_grad, top_offset_grad, edge_scale_grad, top_scale_grad)
        totals = tuple([earlier + latest for earlier, latest in zip(totals, terms)])
        halo_grad = table_grad[MESH_DEV:].reshape(N_MESH, HALO, D).astype(jnp.bfloat16)
        return (totals, (upper_rows, middle_grad, table_grad[:MESH_DEV], halo_grad))
    square_zero = jnp.zeros((D, D), jnp.float32)
    vector_zero = jnp.zeros((D,), jnp.float32)
    start = (square_zero, square_zero, square_zero, square_zero, square_zero, vector_zero, vector_zero, vector_zero, vector_zero)
    upper_totals, outputs = lax.scan(processor_step, start, jnp.arange(blocks))
    upper_all, middle_part, local_grad, halo_grad = outputs
    receiver_ids = jnp.arange(blocks)[:, None, None]
    peer_grid = receiver_ids // N_MESH * N_MESH + jnp.arange(N_MESH)[None, :, None]
    halo_position = halo_rows[peer_grid, receiver_ids % N_MESH, halo_range[None, None, :]]
    flat_position = (peer_grid * MESH_DEV + halo_position).reshape(-1)
    returned = jax.ops.segment_sum(halo_grad.reshape(-1, D).astype(jnp.float32), flat_position, num_segments=blocks * MESH_DEV)
    sender_half = (local_grad.reshape(-1, D) + returned).astype(jnp.bfloat16)
    middle_flat = middle_all.reshape(-1, D)
    middle_total = (middle_part.reshape(-1, D) + through_weight(sender_half, weights[6])).reshape(blocks, MESH_DEV, D)
    sender_weight_grad = row_contract(middle_flat, sender_half)

    def encoder_step(totals, block_id):
        parts = encoder_parts(block_id)
        present, target_index, node_rows, grid_summed, grid_hidden, grid_normed, grid_inverse = parts[:7]
        grid_gathered, low_summed, low_hidden, low_normed, low_inverse = parts[7:12]
        upstream = middle_total[block_id]
        low_grad, low_weight_grad, low_offset_grad, low_scale_grad = perceptron_back(upstream, low_summed, biases[1], weights[5], norm_gains[1], low_hidden, low_normed, low_inverse)
        lower_grad = upstream + through_weight(low_grad, weights[3])
        gathered_grad = through_weight(low_grad, weights[4])
        edge_grad, edge_weight_grad, edge_offset_grad, edge_scale_grad = perceptron_back(gathered_grad[target_index] * present, grid_summed, biases[0], weights[2], norm_gains[0], grid_hidden, grid_normed, grid_inverse)
        edge_float = edge_grad.astype(jnp.float32)
        receiver_half = jax.ops.segment_sum(edge_float, target_index, num_segments=MESH_DEV).astype(jnp.bfloat16)
        slot_grad = lax.optimization_barrier(jnp.sum(edge_float.reshape(FAN, N_GRID, CAP, D), axis=0)).astype(jnp.bfloat16)
        lower_grad = lower_grad + through_weight(receiver_half, weights[1])
        terms = (row_contract(node_rows, receiver_half), edge_weight_grad, row_contract(node_rows, low_grad), row_contract(grid_gathered, low_grad), low_weight_grad, edge_offset_grad, low_offset_grad, edge_scale_grad, low_scale_grad)
        totals = tuple([earlier + latest for earlier, latest in zip(totals, terms)])
        return (totals, (lower_grad, slot_grad))
    lower_totals, outputs = lax.scan(encoder_step, start, jnp.arange(blocks))
    lower_grad_all, slot_grad_all = outputs
    dest_ids = jnp.arange(blocks)[:, None, None]
    source_ids = jnp.arange(N_GRID)[None, :, None] * N_MESH + dest_ids % N_MESH
    slot_position = grid_send_rows[source_ids, dest_ids // N_MESH, slot_range[None, None, :]]
    flat_slots = (source_ids * GRID_DEV + slot_position).reshape(-1)
    grid_half = jax.ops.segment_sum(slot_grad_all.reshape(-1, D).astype(jnp.float32), flat_slots, num_segments=blocks * GRID_DEV).astype(jnp.bfloat16)
    grid_grad = through_weight(grid_half, weights[0])
    mesh_grad = lower_grad_all.reshape(-1, D)
    buckets = [pack_bucket(row_contract(grid_latent, grid_half), lower_totals[0], lower_totals[1], lower_totals[5], lower_totals[7]), pack_bucket(lower_totals[2], lower_totals[3], lower_totals[4], lower_totals[6], lower_totals[8]), pack_bucket(sender_weight_grad, upper_totals[0], upper_totals[1], upper_totals[5], upper_totals[7]), pack_bucket(upper_totals[2], upper_totals[3], upper_totals[4], upper_totals[6], upper_totals[8])]
    grad_scale = 1.0 / math.sqrt(MESH_DEV * blocks)
    weight_grad = jnp.stack(buckets) * grad_scale
    return (upper_all.reshape(-1, D), grid_grad, mesh_grad, weight_grad)
```

```python
import functools
import math

import jax
import jax.numpy as jnp
import numpy as np
from jax import lax
from jax.experimental import pallas as pl
from jax.experimental.pallas import tpu as pltpu
from jax.sharding import PartitionSpec as P

bf16 = jnp.bfloat16
f32 = jnp.float32
epsilon = 1e-05
MESH = pl.DeviceIdType.MESH
PARTS = (2, 4, 2, 4, 4)


def mm(left, right):
    return jnp.dot(left, right, preferred_element_type=f32)


def tn(left, right):
    return lax.dot_general(left, right, (((0,), (0,)), ((), ())), preferred_element_type=f32)


def nt(left, right):
    return lax.dot_general(left, right, (((1,), (1,)), ((), ())), preferred_element_type=f32)


def row_mean(values):
    return jnp.mean(values, axis=-1, keepdims=True)


def column_sum(values):
    return jnp.sum(values, axis=0, keepdims=True)


def forward(x, out_weight):
    sigmoid = 0.5 * jnp.tanh(0.5 * x) + 0.5
    active = x * sigmoid
    slope = active * (1.0 - sigmoid) + sigmoid
    hidden = active.astype(bf16)
    projected = mm(hidden, out_weight)
    centered = projected - row_mean(projected)
    reciprocal = lax.rsqrt(row_mean(centered * centered) + epsilon)
    return hidden, slope, centered * reciprocal, reciprocal


def backward(upstream, gain, normed, reciprocal, slope, out_weight):
    gain_grad = column_sum(upstream * normed)
    weighted = upstream * gain
    inner = reciprocal * (weighted - row_mean(weighted) - normed * row_mean(weighted * normed))
    inner = inner.astype(bf16)
    summed_grad = nt(inner, out_weight) * slope
    return summed_grad.astype(bf16), inner, column_sum(summed_grad), gain_grad


def sizes(grid_dev, mesh_dev, features, edges, cap, fan):
    zh, ny, nc, zl, nx = PARTS
    own = 3 * features // (zh * ny * nc * zl * nx)
    pad = -(-own // 8) * 8
    return dict(
        G=grid_dev, M=mesh_dev, D=features, E=edges, cap=cap, fan=fan, zh=zh, ny=ny, nc=nc, zl=zl, nx=nx,
        nz=zh * zl, ng=zh * ny * nc, nm=zl * nx, own=own, pad=pad, out=-(-(own + 2) // 8) * 8,
        block=3 * features // (zh * ny * nc), plane=zh * zl * own,
    )


def constants(s):
    slots = s["ng"] * s["cap"]
    at = np.arange(slots)
    spread = (at[None, :] % s["cap"] == np.arange(s["cap"])[:, None]).astype(np.float32)
    mask = (at[None, :] // s["cap"] == np.arange(s["ng"])[:, None]).astype(np.float32)
    depth = (at % s["cap"]).astype(np.float32)[None, :]
    rows = s["nx"] * s["nz"] * s["own"]
    perm = np.zeros((rows, rows), np.float32)
    low = np.zeros((s["nz"] * 2 * s["pad"], s["plane"]), np.float32)
    high = np.zeros_like(low)
    for z in range(s["nz"]):
        for i in range(s["own"]):
            for x in range(s["nx"]):
                perm[x * s["plane"] + z * s["own"] + i, (z * s["nx"] + x) * s["own"] + i] = 1
            low[z * 2 * s["pad"] + i, z * s["own"] + i] = 1
            high[z * 2 * s["pad"] + s["pad"] + i, z * s["own"] + i] = 1
    return (
        jnp.asarray(spread, bf16), jnp.asarray(mask, f32), jnp.asarray(depth, f32),
        jnp.asarray(perm, bf16), jnp.asarray(low, bf16), jnp.asarray(high, bf16),
    )


def copies(s):
    kinds = dict(
        a2a=2 * (s["ng"] - 1) + 2 * (s["nm"] - 1), core=4, first=4 * (s["ny"] + s["nx"] - 2),
        second=4 * (s["ny"] + s["nx"] - 2), last=2 * (s["nz"] - 1),
        vec=1 + s["ny"] - 1 + s["nx"] - 1 + s["nz"] - 1, shift=1,
    )
    return sum(kinds.values())


def kernel(
    s, scale,
    grid_latent, mesh_latent, cotangent, weights, biases, gains, send_rows, counts, targets, senders, receivers,
    halo_rows, spread, mask, depth, perm, low_pad, high_pad,
    mesh_out, grid_grad, mesh_grad, shares,
    w, send_hot, target_hot, halo_hot, edge_hot,
    slot_out, slot_in, halo_out, halo_in, back_out, back_in, slot_back_out, slot_back_in,
    slot_terms, hidden0, slope0, normed0, recip0, inner0, slot_sum, gather_sum, receiver_sum,
    table, hidden2, slope2, normed2, recip2, inner2, grad2,
    bucket, core_in, split, first_in, partial, second_in, plane, last_out, last_in,
    vec, vec_sum, vec_in, shift_out, shift_in,
    weight_sem, send_sem, recv_sem,
):
    D, M, cap, fan = s["D"], s["M"], s["cap"], s["fan"]
    zh, ny, nc, zl, nx, nz, ng, nm = (s[k] for k in ("zh", "ny", "nc", "zl", "nx", "nz", "ng", "nm"))
    gi, mi = lax.axis_index("grid"), lax.axis_index("mesh")
    core = gi % nc
    y = (gi // nc) % ny
    z_hi = gi // (nc * ny)
    x = mi % nx
    z_lo = mi // nx
    z = z_hi * zl + z_lo
    flat = gi * nm + mi
    total = ng * nm

    def at_core(o):
        return ((z_hi * ny + y) * nc + (core + o) % nc, mi)

    def at_y(o):
        return ((z_hi * ny + (y + o) % ny) * nc + core, mi)

    def at_x(o):
        return (gi, z_lo * nx + (x + o) % nx)

    def at_z(o):
        to = (z + o) % nz
        return (((to // zl) * ny + y) * nc + core, (to % zl) * nx + x)

    def at_flat(o):
        to = (flat + o + total) % total
        return (to // nm, to % nm)

    order = (1, 3, 0, 2, 4, 5, 6, 7, 9, 8, 10, 11)
    loads = {i: pltpu.make_async_copy(weights.at[i], w.at[i], weight_sem.at[i]) for i in order}
    for i in order:
        loads[i].start()

    barrier = pltpu.get_barrier_semaphore()
    greeted = [((gi + o) % ng, mi) for o in range(1, ng)] + [(gi, (mi + o) % nm) for o in range(1, nm)]
    for a in range(1, zh):
        for b in range(1, zl):
            greeted.append(
                ((((z_hi + a) % zh) * ny + y) * nc + core, ((z_lo + b) % zl) * nx + x)
            )
    greeted += [at_flat(1), at_flat(-1)]
    for device in greeted:
        pl.semaphore_signal(barrier, inc=1, device_id=device, device_id_type=MESH)

    ids = iter(range(copies(s)))
    started = []

    def send(source, target, device):
        i = next(ids)
        copy = pltpu.make_async_remote_copy(
            src_ref=source, dst_ref=target, send_sem=send_sem.at[i], recv_sem=recv_sem.at[i],
            device_id=device, device_id_type=MESH,
        )
        copy.start()
        started.append(copy)
        return copy

    def arrive(batch):
        for copy in batch:
            copy.wait_recv()

    def exchange_grid(out, into):
        batch = [send(out.at[(gi + o) % ng], into.at[gi], ((gi + o) % ng, mi)) for o in range(1, ng)]
        into[pl.ds(gi, 1)] = out[pl.ds(gi, 1)]
        return batch

    def exchange_mesh(out, into):
        batch = [send(out.at[(mi + o) % nm], into.at[mi], (gi, (mi + o) % nm)) for o in range(1, nm)]
        into[pl.ds(mi, 1)] = out[pl.ds(mi, 1)]
        return batch

    def lay(values):
        spread_out = mm(values.astype(f32).astype(bf16), spread[...])
        return column_sum(spread_out * mask[...])

    def one_hot(rows, nodes):
        node = lax.broadcasted_iota(jnp.int32, (nodes, rows.shape[1]), 0).astype(f32)
        return jnp.where(node == rows, 1.0, 0.0).astype(bf16)

    send_hot[...] = one_hot(lay(send_rows[0]), s["G"])
    slot_out[...] = tn(send_hot[...], grid_latent[...]).astype(bf16).reshape(slot_out.shape)
    pl.semaphore_wait(barrier, len(greeted))
    slots_batch = exchange_grid(slot_out, slot_in)

    count_row = mm(counts[...].astype(f32).astype(bf16), mask[...].astype(bf16))
    live = depth[...] < count_row
    for k in range(fan):
        target_hot[k] = one_hot(jnp.where(live, lay(targets[0, k]), -1.0), M)
    halo_hot[...] = one_hot(lay(halo_rows[0]), M)
    tiles, _, tile = edge_hot.shape
    joined = M + nm * cap
    for t in range(tiles):
        part = pl.ds(t * tile, tile)
        edge_hot[t, :joined] = one_hot(senders[:, part].astype(f32), joined)
        edge_hot[t, joined:] = one_hot(receivers[:, part].astype(f32), M)

    loads[1].wait()
    latent = mesh_latent[...]
    receiver_terms = mm(latent, w[1]).astype(bf16)
    loads[3].wait()
    low_part = mm(latent, w[3])
    loads[0].wait()
    loads[2].wait()

    arrive(slots_batch)
    slot_terms[...] = mm(slot_in[...].reshape(ng * cap, D), w[0]).astype(bf16)
    gather_sum[...] = jnp.zeros_like(gather_sum)

    def encode(k, carry):
        hot = target_hot[k]
        x0 = slot_terms[...].astype(f32) + tn(hot, receiver_terms) + biases[0:1, :]
        hidden, slope, normed, recip = forward(x0, w[2])
        hidden0[k] = hidden
        slope0[k] = slope
        normed0[k] = normed
        recip0[k] = recip
        gather_sum[...] += mm(hot, (normed * gains[0:1, :]).astype(bf16))
        return carry

    lax.fori_loop(0, fan, encode, 0)
    grid_gathered = gather_sum[...].astype(bf16)

    loads[4].wait()
    loads[5].wait()
    x1 = low_part + mm(grid_gathered, w[4]) + biases[1:2, :]
    hidden1, slope1, normed1, recip1 = forward(x1, w[5])
    middle = (latent.astype(f32) + normed1 * gains[1:2, :]).astype(bf16)
    halo_out[...] = tn(halo_hot[...], middle).astype(bf16).reshape(halo_out.shape)
    halo_batch = exchange_mesh(halo_out, halo_in)

    for i in (6, 7, 9, 8):
        loads[i].wait()
    table[:M] = mm(middle, w[6]).astype(bf16)
    table[joined:] = mm(middle, w[7]).astype(bf16)
    top_part = mm(middle, w[9]) + biases[3:4, :]

    arrive(halo_batch)
    halo_rows_in = halo_in[...].reshape(nm * cap, D)
    table[M:joined] = mm(halo_rows_in, w[6]).astype(bf16)
    gather_sum[...] = jnp.zeros_like(gather_sum)

    def process(t, carry):
        x2 = tn(edge_hot[t], table[...]) + biases[2:3, :]
        hidden, slope, normed, recip = forward(x2, w[8])
        hidden2[t] = hidden
        slope2[t] = slope
        normed2[t] = normed
        recip2[t] = recip
        gather_sum[...] += mm(edge_hot[t, joined:], (normed * gains[2:3, :]).astype(bf16))
        return carry

    lax.fori_loop(0, tiles, process, 0)
    mesh_gathered = gather_sum[...].astype(bf16)

    loads[10].wait()
    loads[11].wait()
    x3 = top_part + mm(mesh_gathered, w[10])
    hidden3, slope3, normed3, recip3 = forward(x3, w[11])
    mesh_out[...] = (middle.astype(f32) + normed3 * gains[3:4, :]).astype(bf16)
    upstream = cotangent[...].astype(f32)
    grad3, inner3, bias_grad, gain_grad = backward(upstream, gains[3:4, :], normed3, recip3, slope3, w[11])
    vec[6:7, :] = bias_grad
    vec[7:8, :] = gain_grad
    gathered_grad = nt(grad3, w[10]).astype(bf16)
    middle_part = upstream + nt(grad3, w[9])

    def put(j, m, value):
        value = value.astype(bf16)
        for r in range(0, D, 32):
            a, rest = divmod(m * D + r, ny * nc * s["block"])
            b, rest = divmod(rest, nc * s["block"])
            c, q = divmod(rest, s["block"])
            bucket[j, c, b, a * s["block"] + q : a * s["block"] + q + 32, :] = value[r : r + 32]

    half = D // 2
    rows = s["plane"]
    waiting = {}

    def core_start(j):
        waiting["core", j] = [send(bucket.at[j, 1 - core], core_in.at[j], at_core(1))]

    def first_start(j):
        arrive(waiting["core", j])

        def fold(b, carry):
            both = bucket[j, core, b].astype(f32) + core_in[j, b].astype(f32)
            moved = mm(perm[...], both.astype(bf16)).astype(bf16)
            for a in range(nx):
                split[j, 0, b, a] = moved[a * rows : (a + 1) * rows, :half]
                split[j, 1, a, b] = moved[a * rows : (a + 1) * rows, half:]
            return carry

        lax.fori_loop(0, ny, fold, 0)
        waiting["first", j] = [
            send(split.at[j, 0, (y + o) % ny], first_in.at[j, 0, o - 1], at_y(o)) for o in range(1, ny)
        ] + [send(split.at[j, 1, (x + o) % nx], first_in.at[j, 1, o - 1], at_x(o)) for o in range(1, nx)]

    def second_start(j):
        arrive(waiting["first", j])
        for h, mine, n in ((0, y, ny), (1, x, nx)):
            value = split[j, h, mine].astype(f32)
            for o in range(n - 1):
                value = value + first_in[j, h, o].astype(f32)
            partial[j, h] = value.astype(bf16)
        waiting["second", j] = [
            send(partial.at[j, 0, (x + o) % nx], second_in.at[j, 0, o - 1], at_x(o)) for o in range(1, nx)
        ] + [send(partial.at[j, 1, (y + o) % ny], second_in.at[j, 1, o - 1], at_y(o)) for o in range(1, ny)]

    def second_finish(j):
        arrive(waiting["second", j])
        for h, mine, n in ((0, x, nx), (1, y, ny)):
            value = partial[j, h, mine].astype(f32)
            for o in range(n - 1):
                value = value + second_in[j, h, o].astype(f32)
            plane[j, :, h * half : (h + 1) * half] = value.astype(bf16)

    def last_start(p):
        padded = mm(low_pad[...], plane[2 * p]) + mm(high_pad[...], plane[2 * p + 1])
        last_out[p] = padded.astype(bf16).reshape(last_out.shape[1:])
        waiting["last", p] = [
            send(last_out.at[p, (z + o) % nz], last_in.at[p, o - 1], at_z(o)) for o in range(1, nz)
        ]

    def last_finish(p):
        arrive(waiting["last", p])
        value = last_out[p, z].astype(f32)
        for o in range(nz - 1):
            value = value + last_in[p, o].astype(f32)
        return value * scale

    put(3, 0, tn(middle, grad3))
    put(3, 1, tn(mesh_gathered, grad3))
    put(3, 2, tn(hidden3, inner3))
    core_start(3)

    vec[4:6, :] = jnp.zeros((2, D), f32)

    def process_back(t, carry):
        up = tn(edge_hot[t, joined:], gathered_grad)
        grad, inner, bias_part, gain_part = backward(up, gains[2:3, :], normed2[t], recip2[t], slope2[t], w[8])
        inner2[t] = inner
        grad2[t] = grad
        vec[4:5, :] += bias_part
        vec[5:6, :] += gain_part
        return carry

    lax.fori_loop(0, tiles, process_back, 0)
    spread_grad = mm(edge_hot[0], grad2[0])
    for t in range(1, tiles):
        spread_grad = spread_grad + mm(edge_hot[t], grad2[t])
    spread_half = spread_grad.astype(bf16)
    back_out[...] = spread_half[M:joined].reshape(back_out.shape)
    back_batch = exchange_mesh(back_out, back_in)
    receiver_half = spread_half[joined:]
    first_start(3)
    put(2, 0, tn(middle, spread_half[:M]) + tn(halo_rows_in, spread_half[M:joined]))
    put(2, 1, tn(middle, receiver_half))
    put(2, 2, tn(hidden2[...].reshape(tiles * tile, D), inner2[...].reshape(tiles * tile, D)))
    core_start(2)
    middle_part = middle_part + nt(receiver_half, w[7])
    arrive(back_batch)
    returned = mm(halo_hot[...], back_in[...].reshape(nm * cap, D))
    sender_half = (spread_grad[:M] + returned).astype(bf16)
    middle_grad = middle_part + nt(sender_half, w[6])

    grad1, inner1, bias_grad, gain_grad = backward(middle_grad, gains[1:2, :], normed1, recip1, slope1, w[5])
    vec[2:3, :] = bias_grad
    vec[3:4, :] = gain_grad
    low_gathered_grad = nt(grad1, w[4]).astype(bf16)
    lower_part = middle_grad + nt(grad1, w[3])
    put(1, 0, tn(latent, grad1))
    put(1, 1, tn(grid_gathered, grad1))
    put(1, 2, tn(hidden1, inner1))
    core_start(1)
    first_start(2)
    second_start(3)

    vec[0:2, :] = jnp.zeros((2, D), f32)
    slot_sum[...] = jnp.zeros_like(slot_sum)
    receiver_sum[...] = jnp.zeros_like(receiver_sum)

    def encode_back(k, carry):
        hot = target_hot[k]
        up = tn(hot, low_gathered_grad)
        grad, inner, bias_part, gain_part = backward(up, gains[0:1, :], normed0[k], recip0[k], slope0[k], w[2])
        inner0[k] = inner
        slot_sum[...] += grad.astype(f32)
        receiver_sum[...] += mm(hot, grad)
        vec[0:1, :] += bias_part
        vec[1:2, :] += gain_part
        return carry

    lax.fori_loop(0, fan, encode_back, 0)
    slot_half = slot_sum[...].astype(bf16)
    slot_back_out[...] = slot_half.reshape(slot_back_out.shape)
    slot_back_batch = exchange_grid(slot_back_out, slot_back_in)
    waiting["vec", 0] = [send(vec, vec_in.at[0], at_core(1))]
    receiver_low = receiver_sum[...].astype(bf16)
    put(0, 0, tn(slot_in[...].reshape(ng * cap, D), slot_half))
    put(0, 1, tn(latent, receiver_low))
    put(0, 2, tn(hidden0[...].reshape(fan * ng * cap, D), inner0[...].reshape(fan * ng * cap, D)))
    core_start(0)
    first_start(1)
    second_start(2)
    second_finish(3)
    mesh_grad[...] = lower_part + nt(receiver_low, w[1])
    first_start(0)

    at = 0

    def vec_step(batch_key, level, steps, start):
        arrive(waiting[batch_key])
        value = vec[...] if level == 0 else vec_sum[level - 1]
        for o in steps:
            value = value + vec_in[o]
        return value

    vec_sum[0] = vec_step(("vec", 0), 0, range(0, 1), 0)
    waiting["vec", 1] = [send(vec_sum.at[0], vec_in.at[o], at_y(o)) for o in range(1, ny)]
    second_finish(2)
    last_start(1)
    second_start(1)
    vec_sum[1] = vec_step(("vec", 1), 1, range(1, ny), 0)
    waiting["vec", 2] = [send(vec_sum.at[1], vec_in.at[ny - 1 + o], at_x(o)) for o in range(1, nx)]

    arrive(slot_back_batch)
    grid_half = mm(send_hot[...], slot_back_in[...].reshape(ng * cap, D)).astype(bf16)
    grid_grad[...] = nt(grid_half, w[0])

    second_start(0)
    vec_sum[2] = vec_step(("vec", 2), 2, range(ny, ny + nx - 1), 0)
    base = ny + nx - 2
    waiting["vec", 3] = [send(vec_sum.at[2], vec_in.at[base + o], at_z(o)) for o in range(1, nz)]
    second_finish(1)
    second_finish(0)
    last_start(0)
    upper = last_finish(1)
    vec_total = vec_step(("vec", 3), 3, range(base + 1, base + nz), 0) * scale
    lower = last_finish(0)
    pad = s["pad"]
    results = (lower[:pad], lower[pad:], upper[:pad], upper[pad:])
    first_device = flat == 0
    for j in range(4):
        shift_out[2 * j : 2 * j + 2, :] = jnp.where(first_device, vec_total[2 * j : 2 * j + 2], results[j][:2])
    shift = send(shift_out, shift_in, at_flat(-1))
    own = s["own"]
    for j in range(4):
        shares[j, :own, :] = results[j][:own]
    arrive([shift])
    for j in range(4):
        shares[j, own : own + 2, :] = shift_in[2 * j : 2 * j + 2, :]
    for copy in started:
        copy.wait_send()


def local(grid_latent, mesh_latent, mesh_cotangent, weights, biases, norm_gains, send_rows, counts, targets,
          senders, receivers, halo_rows):
    G, D = grid_latent.shape
    M = mesh_latent.shape[0]
    fan, sources, cap = targets.shape[1:]
    E = senders.shape[1]
    s = sizes(G, M, D, E, cap, fan)
    ng, nm, ny, nx, nz = s["ng"], s["nm"], s["ny"], s["nx"], s["nz"]
    slots = ng * cap
    tiles = 2
    tile = E // tiles
    joined = M + nm * cap
    half = D // 2
    n = copies(s)
    scale = 1.0 / math.sqrt(M * ng * nm)
    vmem = pl.BlockSpec(memory_space=pltpu.VMEM)
    scratch = [
        pltpu.VMEM(weights.shape, bf16),
        pltpu.VMEM((G, slots), bf16), pltpu.VMEM((fan, M, slots), bf16), pltpu.VMEM((M, nm * cap), bf16),
        pltpu.VMEM((tiles, joined + M, tile), bf16),
        pltpu.VMEM((ng, cap, D), bf16), pltpu.VMEM((ng, cap, D), bf16),
        pltpu.VMEM((nm, cap, D), bf16), pltpu.VMEM((nm, cap, D), bf16),
        pltpu.VMEM((nm, cap, D), bf16), pltpu.VMEM((nm, cap, D), bf16),
        pltpu.VMEM((ng, cap, D), bf16), pltpu.VMEM((ng, cap, D), bf16),
        pltpu.VMEM((slots, D), bf16),
        pltpu.VMEM((fan, slots, D), bf16), pltpu.VMEM((fan, slots, D), f32), pltpu.VMEM((fan, slots, D), f32),
        pltpu.VMEM((fan, slots, 1), f32), pltpu.VMEM((fan, slots, D), bf16),
        pltpu.VMEM((slots, D), f32), pltpu.VMEM((M, D), f32), pltpu.VMEM((M, D), f32),
        pltpu.VMEM((joined + M, D), bf16),
        pltpu.VMEM((tiles, tile, D), bf16), pltpu.VMEM((tiles, tile, D), f32), pltpu.VMEM((tiles, tile, D), f32),
        pltpu.VMEM((tiles, tile, 1), f32), pltpu.VMEM((tiles, tile, D), bf16), pltpu.VMEM((tiles, tile, D), bf16),
        pltpu.VMEM((4, 2, ny, s["zh"] * s["block"], D), bf16),
        pltpu.VMEM((4, ny, s["zh"] * s["block"], D), bf16),
        pltpu.VMEM((4, 2, nx, nx, s["plane"], half), bf16),
        pltpu.VMEM((4, 2, nx - 1, nx, s["plane"], half), bf16),
        pltpu.VMEM((4, 2, nx, s["plane"], half), bf16),
        pltpu.VMEM((4, 2, nx - 1, s["plane"], half), bf16),
        pltpu.VMEM((4, s["plane"], D), bf16),
        pltpu.VMEM((2, nz, 2 * s["pad"], D), bf16),
        pltpu.VMEM((2, nz - 1, 2 * s["pad"], D), bf16),
        pltpu.VMEM((8, D), f32), pltpu.VMEM((3, 8, D), f32), pltpu.VMEM((ny + nx + nz - 2, 8, D), f32),
        pltpu.VMEM((8, D), f32), pltpu.VMEM((8, D), f32),
        pltpu.SemaphoreType.DMA((weights.shape[0],)),
        pltpu.SemaphoreType.DMA((n,)), pltpu.SemaphoreType.DMA((n,)),
    ]
    mesh_out, grid_grad, mesh_grad, shares = pl.pallas_call(
        functools.partial(kernel, s, scale),
        out_shape=(
            jax.ShapeDtypeStruct((M, D), bf16), jax.ShapeDtypeStruct((G, D), f32),
            jax.ShapeDtypeStruct((M, D), f32), jax.ShapeDtypeStruct((4, s["out"], D), f32),
        ),
        in_specs=[vmem] * 3 + [pl.BlockSpec(memory_space=pl.ANY)] + [vmem] * 14,
        out_specs=(vmem,) * 4,
        scratch_shapes=scratch,
        compiler_params=pltpu.CompilerParams(
            collective_id=0, has_side_effects=True, vmem_limit_bytes=60 * 1024 * 1024
        ),
    )(
        grid_latent, mesh_latent, mesh_cotangent, weights, biases, norm_gains, send_rows, counts, targets,
        senders, receivers, halo_rows, *constants(s),
    )
    extra = 2 * D // (ng * nm)
    start = (lax.axis_index("grid") * nm + lax.axis_index("mesh")) * extra
    weight_grad = lax.dynamic_slice(
        shares.reshape(4, s["out"] * D), (0, start), (4, s["own"] * D + extra)
    )
    return mesh_out, grid_grad, mesh_grad, weight_grad


def solution(mesh):
    both = ("grid", "mesh")
    placed = (
        P(both, None), P(both, None), P(both, None), P(), P(), P(), P(both, None, None), P(both, None),
        P(both, None, None, None), P(both, None), P(both, None), P(both, None, None),
    )
    return jax.shard_map(
        local, mesh=mesh, in_specs=placed,
        out_specs=(P(both, None), P(both, None), P(both, None), P(None, both)),
        check_vma=False,
    )
```

```python
import functools
import math

import jax
import jax.numpy as jnp
import numpy as np
from jax import lax
from jax.experimental import pallas as pl
from jax.experimental.pallas import tpu as pltpu
from jax.sharding import PartitionSpec as P

bf16 = jnp.bfloat16
f32 = jnp.float32
epsilon = 1e-05
MESH = pl.DeviceIdType.MESH
PARTS = (2, 4, 2, 4, 4)


def mm(left, right):
    return jnp.dot(left, right, preferred_element_type=f32)


def tn(left, right):
    return lax.dot_general(left, right, (((0,), (0,)), ((), ())), preferred_element_type=f32)


def nt(left, right):
    return lax.dot_general(left, right, (((1,), (1,)), ((), ())), preferred_element_type=f32)


def row_mean(values):
    return jnp.mean(values, axis=-1, keepdims=True)


def column_sum(values):
    return jnp.sum(values, axis=0, keepdims=True)


def forward(x, out_weight):
    sigmoid = 0.5 * jnp.tanh(0.5 * x) + 0.5
    active = x * sigmoid
    slope = active * (1.0 - sigmoid) + sigmoid
    hidden = active.astype(bf16)
    projected = mm(hidden, out_weight)
    centered = projected - row_mean(projected)
    reciprocal = lax.rsqrt(row_mean(centered * centered) + epsilon)
    return hidden, slope, centered * reciprocal, reciprocal


def backward(upstream, gain, normed, reciprocal, slope, out_weight):
    gain_grad = column_sum(upstream * normed)
    weighted = upstream * gain
    inner = reciprocal * (weighted - row_mean(weighted) - normed * row_mean(weighted * normed))
    inner = inner.astype(bf16)
    summed_grad = nt(inner, out_weight) * slope
    return summed_grad.astype(bf16), inner, column_sum(summed_grad), gain_grad


def sizes(grid_dev, mesh_dev, features, edges, cap, fan):
    zh, ny, nc, zl, nx = PARTS
    own = 3 * features // (zh * ny * nc * zl * nx)
    pad = -(-own // 8) * 8
    return dict(
        G=grid_dev, M=mesh_dev, D=features, E=edges, cap=cap, fan=fan, zh=zh, ny=ny, nc=nc, zl=zl, nx=nx,
        nz=zh * zl, ng=zh * ny * nc, nm=zl * nx, own=own, pad=pad, out=-(-(own + 2) // 8) * 8,
        block=3 * features // (zh * ny * nc), plane=zh * zl * own,
    )


def constants(s):
    slots = s["ng"] * s["cap"]
    at = np.arange(slots)
    spread = (at[None, :] % s["cap"] == np.arange(s["cap"])[:, None]).astype(np.float32)
    mask = (at[None, :] // s["cap"] == np.arange(s["ng"])[:, None]).astype(np.float32)
    depth = (at % s["cap"]).astype(np.float32)[None, :]
    rows = s["nx"] * s["nz"] * s["own"]
    perm = np.zeros((rows, rows), np.float32)
    low = np.zeros((s["nz"] * 2 * s["pad"], s["plane"]), np.float32)
    high = np.zeros_like(low)
    for z in range(s["nz"]):
        for i in range(s["own"]):
            for x in range(s["nx"]):
                perm[x * s["plane"] + z * s["own"] + i, (z * s["nx"] + x) * s["own"] + i] = 1
            low[z * 2 * s["pad"] + i, z * s["own"] + i] = 1
            high[z * 2 * s["pad"] + s["pad"] + i, z * s["own"] + i] = 1
    return (
        jnp.asarray(spread, f32), jnp.asarray(mask, f32), jnp.asarray(depth, f32),
        jnp.asarray(perm, f32), jnp.asarray(low, f32), jnp.asarray(high, f32),
    )


def copies(s):
    kinds = dict(
        a2a=2 * (s["ng"] - 1) + 2 * (s["nm"] - 1), core=4, first=4 * (s["ny"] + s["nx"] - 2),
        second=4 * (s["ny"] + s["nx"] - 2), last=2 * (s["nz"] - 1),
        vec=1 + s["ny"] - 1 + s["nx"] - 1 + s["nz"] - 1, shift=1,
    )
    return sum(kinds.values())


def kernel(
    s, scale,
    sources, weights, mesh_out_hbm, grid_grad_hbm, mesh_grad_hbm, shares_hbm,
    grid_latent, mesh_latent, cotangent, biases, gains, send_rows, counts, targets, senders, receivers,
    halo_rows, spread, mask, depth, perm, low_pad, high_pad,
    mesh_out, grid_grad, mesh_grad, shares,
    w, send_hot, target_hot, halo_hot, edge_hot,
    slot_out, slot_in, halo_out, halo_in, back_out, back_in, slot_back_out, slot_back_in,
    slot_terms, hidden0, slope0, normed0, recip0, inner0, slot_sum, gather_sum, receiver_sum,
    table, hidden2, slope2, normed2, recip2, inner2, grad2,
    bucket, core_in, split, first_in, partial, second_in, plane, last_out, last_in,
    vec, vec_sum, vec_in, shift_out, shift_in,
    weight_sem, input_sem, output_sem, send_sem, recv_sem,
):
    D, M, cap, fan = s["D"], s["M"], s["cap"], s["fan"]
    zh, ny, nc, zl, nx, nz, ng, nm = (s[k] for k in ("zh", "ny", "nc", "zl", "nx", "nz", "ng", "nm"))
    gi, mi = lax.axis_index("grid"), lax.axis_index("mesh")
    core = gi % nc
    y = (gi // nc) % ny
    z_hi = gi // (nc * ny)
    x = mi % nx
    z_lo = mi // nx
    z = z_hi * zl + z_lo
    flat = gi * nm + mi
    total = ng * nm

    def at_core(o):
        return ((z_hi * ny + y) * nc + (core + o) % nc, mi)

    def at_y(o):
        return ((z_hi * ny + (y + o) % ny) * nc + core, mi)

    def at_x(o):
        return (gi, z_lo * nx + (x + o) % nx)

    def at_z(o):
        to = (z + o) % nz
        return (((to // zl) * ny + y) * nc + core, (to % zl) * nx + x)

    def at_flat(o):
        to = (flat + o + total) % total
        return (to // nm, to % nm)

    operands = (
        send_rows, spread, mask, grid_latent, counts, depth, targets, halo_rows, senders, receivers,
        mesh_latent, biases, gains, cotangent, perm, low_pad, high_pad,
    )
    fetch = [pltpu.make_async_copy(a, b, input_sem.at[i]) for i, (a, b) in enumerate(zip(sources, operands))]
    for copy in fetch:
        copy.start()
    results_out = []

    def store(value_ref, target):
        copy = pltpu.make_async_copy(value_ref, target, output_sem.at[len(results_out)])
        copy.start()
        results_out.append(copy)

    order = (1, 3, 0, 2, 4, 5, 6, 7, 9, 8, 10, 11)
    loads = {i: pltpu.make_async_copy(weights.at[i], w.at[i], weight_sem.at[i]) for i in order}
    for i in order:
        loads[i].start()

    barrier = pltpu.get_barrier_semaphore()
    greeted = [((gi + o) % ng, mi) for o in range(1, ng)] + [(gi, (mi + o) % nm) for o in range(1, nm)]
    for a in range(1, zh):
        for b in range(1, zl):
            greeted.append(
                ((((z_hi + a) % zh) * ny + y) * nc + core, ((z_lo + b) % zl) * nx + x)
            )
    greeted += [at_flat(1), at_flat(-1)]
    for device in greeted:
        pl.semaphore_signal(barrier, inc=1, device_id=device, device_id_type=MESH)

    ids = iter(range(copies(s)))
    started = []

    def send(source, target, device):
        i = next(ids)
        copy = pltpu.make_async_remote_copy(
            src_ref=source, dst_ref=target, send_sem=send_sem.at[i], recv_sem=recv_sem.at[i],
            device_id=device, device_id_type=MESH,
        )
        copy.start()
        started.append(copy)
        return copy

    def arrive(batch):
        for copy in batch:
            copy.wait_recv()

    def exchange_grid(out, into):
        batch = [send(out.at[(gi + o) % ng], into.at[gi], ((gi + o) % ng, mi)) for o in range(1, ng)]
        into[pl.ds(gi, 1)] = out[pl.ds(gi, 1)]
        return batch

    def exchange_mesh(out, into):
        batch = [send(out.at[(mi + o) % nm], into.at[mi], (gi, (mi + o) % nm)) for o in range(1, nm)]
        into[pl.ds(mi, 1)] = out[pl.ds(mi, 1)]
        return batch

    def lay(values):
        spread_out = mm(values.astype(f32).astype(bf16), spread[...].astype(bf16))
        return column_sum(spread_out * mask[...])

    def one_hot(rows, nodes):
        node = lax.broadcasted_iota(jnp.int32, (nodes, rows.shape[1]), 0).astype(f32)
        return jnp.where(node == rows, 1.0, 0.0).astype(bf16)

    for copy in fetch[:4]:
        copy.wait()
    send_hot[...] = one_hot(lay(send_rows[0]), s["G"])
    slot_out[...] = tn(send_hot[...], grid_latent[...]).astype(bf16).reshape(slot_out.shape)
    pl.semaphore_wait(barrier, len(greeted))
    slots_batch = exchange_grid(slot_out, slot_in)

    for copy in fetch[4:]:
        copy.wait()
    count_row = mm(counts[...].astype(f32).astype(bf16), mask[...].astype(bf16))
    live = depth[...] < count_row
    for k in range(fan):
        target_hot[k] = one_hot(jnp.where(live, lay(targets[0, k]), -1.0), M)
    halo_hot[...] = one_hot(lay(halo_rows[0]), M)
    tiles, _, tile = edge_hot.shape
    joined = M + nm * cap
    for t in range(tiles):
        part = pl.ds(t * tile, tile)
        edge_hot[t, :joined] = one_hot(senders[:, part].astype(f32), joined)
        edge_hot[t, joined:] = one_hot(receivers[:, part].astype(f32), M)

    loads[1].wait()
    latent = mesh_latent[...]
    receiver_terms = mm(latent, w[1]).astype(bf16)
    loads[3].wait()
    low_part = mm(latent, w[3])
    loads[0].wait()
    loads[2].wait()

    arrive(slots_batch)
    slot_terms[...] = mm(slot_in[...].reshape(ng * cap, D), w[0]).astype(bf16)
    gather_sum[...] = jnp.zeros_like(gather_sum)

    def encode(k, carry):
        hot = target_hot[k]
        x0 = slot_terms[...].astype(f32) + tn(hot, receiver_terms) + biases[0:1, :]
        hidden, slope, normed, recip = forward(x0, w[2])
        hidden0[k] = hidden
        slope0[k] = slope
        normed0[k] = normed
        recip0[k] = recip
        gather_sum[...] += mm(hot, (normed * gains[0:1, :]).astype(bf16))
        return carry

    lax.fori_loop(0, fan, encode, 0)
    grid_gathered = gather_sum[...].astype(bf16)

    loads[4].wait()
    loads[5].wait()
    x1 = low_part + mm(grid_gathered, w[4]) + biases[1:2, :]
    hidden1, slope1, normed1, recip1 = forward(x1, w[5])
    middle = (latent.astype(f32) + normed1 * gains[1:2, :]).astype(bf16)
    halo_out[...] = tn(halo_hot[...], middle).astype(bf16).reshape(halo_out.shape)
    halo_batch = exchange_mesh(halo_out, halo_in)

    for i in (6, 7, 9, 8):
        loads[i].wait()
    table[:M] = mm(middle, w[6]).astype(bf16)
    table[joined:] = mm(middle, w[7]).astype(bf16)
    top_part = mm(middle, w[9]) + biases[3:4, :]

    arrive(halo_batch)
    halo_rows_in = halo_in[...].reshape(nm * cap, D)
    table[M:joined] = mm(halo_rows_in, w[6]).astype(bf16)
    gather_sum[...] = jnp.zeros_like(gather_sum)

    def process(t, carry):
        x2 = tn(edge_hot[t], table[...]) + biases[2:3, :]
        hidden, slope, normed, recip = forward(x2, w[8])
        hidden2[t] = hidden
        slope2[t] = slope
        normed2[t] = normed
        recip2[t] = recip
        gather_sum[...] += mm(edge_hot[t, joined:], (normed * gains[2:3, :]).astype(bf16))
        return carry

    lax.fori_loop(0, tiles, process, 0)
    mesh_gathered = gather_sum[...].astype(bf16)

    loads[10].wait()
    loads[11].wait()
    x3 = top_part + mm(mesh_gathered, w[10])
    hidden3, slope3, normed3, recip3 = forward(x3, w[11])
    mesh_out[...] = (middle.astype(f32) + normed3 * gains[3:4, :]).astype(bf16)
    store(mesh_out, mesh_out_hbm)
    upstream = cotangent[...].astype(f32)
    grad3, inner3, bias_grad, gain_grad = backward(upstream, gains[3:4, :], normed3, recip3, slope3, w[11])
    vec[6:7, :] = bias_grad
    vec[7:8, :] = gain_grad
    gathered_grad = nt(grad3, w[10]).astype(bf16)
    middle_part = upstream + nt(grad3, w[9])

    def put(j, m, value):
        value = value.astype(bf16)
        for r in range(0, D, 32):
            a, rest = divmod(m * D + r, ny * nc * s["block"])
            b, rest = divmod(rest, nc * s["block"])
            c, q = divmod(rest, s["block"])
            bucket[j, c, b, a * s["block"] + q : a * s["block"] + q + 32, :] = value[r : r + 32]

    half = D // 2
    rows = s["plane"]
    waiting = {}

    def core_start(j):
        waiting["core", j] = [send(bucket.at[j, 1 - core], core_in.at[j], at_core(1))]

    def first_start(j):
        arrive(waiting["core", j])

        def fold(b, carry):
            both = bucket[j, core, b].astype(f32) + core_in[j, b].astype(f32)
            moved = mm(perm[...].astype(bf16), both.astype(bf16)).astype(bf16)
            for a in range(nx):
                split[j, 0, b, a] = moved[a * rows : (a + 1) * rows, :half]
                split[j, 1, a, b] = moved[a * rows : (a + 1) * rows, half:]
            return carry

        lax.fori_loop(0, ny, fold, 0)
        waiting["first", j] = [
            send(split.at[j, 0, (y + o) % ny], first_in.at[j, 0, o - 1], at_y(o)) for o in range(1, ny)
        ] + [send(split.at[j, 1, (x + o) % nx], first_in.at[j, 1, o - 1], at_x(o)) for o in range(1, nx)]

    def second_start(j):
        arrive(waiting["first", j])
        for h, mine, n in ((0, y, ny), (1, x, nx)):
            value = split[j, h, mine].astype(f32)
            for o in range(n - 1):
                value = value + first_in[j, h, o].astype(f32)
            partial[j, h] = value.astype(bf16)
        waiting["second", j] = [
            send(partial.at[j, 0, (x + o) % nx], second_in.at[j, 0, o - 1], at_x(o)) for o in range(1, nx)
        ] + [send(partial.at[j, 1, (y + o) % ny], second_in.at[j, 1, o - 1], at_y(o)) for o in range(1, ny)]

    def second_finish(j):
        arrive(waiting["second", j])
        for h, mine, n in ((0, x, nx), (1, y, ny)):
            value = partial[j, h, mine].astype(f32)
            for o in range(n - 1):
                value = value + second_in[j, h, o].astype(f32)
            plane[j, :, h * half : (h + 1) * half] = value.astype(bf16)

    def last_start(p):
        padded = mm(low_pad[...].astype(bf16), plane[2 * p]) + mm(high_pad[...].astype(bf16), plane[2 * p + 1])
        last_out[p] = padded.astype(bf16).reshape(last_out.shape[1:])
        waiting["last", p] = [
            send(last_out.at[p, (z + o) % nz], last_in.at[p, o - 1], at_z(o)) for o in range(1, nz)
        ]

    def last_finish(p):
        arrive(waiting["last", p])
        value = last_out[p, z].astype(f32)
        for o in range(nz - 1):
            value = value + last_in[p, o].astype(f32)
        return value * scale

    put(3, 0, tn(middle, grad3))
    put(3, 1, tn(mesh_gathered, grad3))
    put(3, 2, tn(hidden3, inner3))
    core_start(3)

    vec[4:6, :] = jnp.zeros((2, D), f32)

    def process_back(t, carry):
        up = tn(edge_hot[t, joined:], gathered_grad)
        grad, inner, bias_part, gain_part = backward(up, gains[2:3, :], normed2[t], recip2[t], slope2[t], w[8])
        inner2[t] = inner
        grad2[t] = grad
        vec[4:5, :] += bias_part
        vec[5:6, :] += gain_part
        return carry

    lax.fori_loop(0, tiles, process_back, 0)
    spread_grad = mm(edge_hot[0], grad2[0])
    for t in range(1, tiles):
        spread_grad = spread_grad + mm(edge_hot[t], grad2[t])
    spread_half = spread_grad.astype(bf16)
    back_out[...] = spread_half[M:joined].reshape(back_out.shape)
    back_batch = exchange_mesh(back_out, back_in)
    receiver_half = spread_half[joined:]
    first_start(3)
    put(2, 0, tn(middle, spread_half[:M]) + tn(halo_rows_in, spread_half[M:joined]))
    put(2, 1, tn(middle, receiver_half))
    put(2, 2, tn(hidden2[...].reshape(tiles * tile, D), inner2[...].reshape(tiles * tile, D)))
    core_start(2)
    middle_part = middle_part + nt(receiver_half, w[7])
    arrive(back_batch)
    returned = mm(halo_hot[...], back_in[...].reshape(nm * cap, D))
    sender_half = (spread_grad[:M] + returned).astype(bf16)
    middle_grad = middle_part + nt(sender_half, w[6])

    grad1, inner1, bias_grad, gain_grad = backward(middle_grad, gains[1:2, :], normed1, recip1, slope1, w[5])
    vec[2:3, :] = bias_grad
    vec[3:4, :] = gain_grad
    low_gathered_grad = nt(grad1, w[4]).astype(bf16)
    lower_part = middle_grad + nt(grad1, w[3])
    put(1, 0, tn(latent, grad1))
    put(1, 1, tn(grid_gathered, grad1))
    put(1, 2, tn(hidden1, inner1))
    core_start(1)
    first_start(2)
    second_start(3)

    vec[0:2, :] = jnp.zeros((2, D), f32)
    slot_sum[...] = jnp.zeros_like(slot_sum)
    receiver_sum[...] = jnp.zeros_like(receiver_sum)

    def encode_back(k, carry):
        hot = target_hot[k]
        up = tn(hot, low_gathered_grad)
        grad, inner, bias_part, gain_part = backward(up, gains[0:1, :], normed0[k], recip0[k], slope0[k], w[2])
        inner0[k] = inner
        slot_sum[...] += grad.astype(f32)
        receiver_sum[...] += mm(hot, grad)
        vec[0:1, :] += bias_part
        vec[1:2, :] += gain_part
        return carry

    lax.fori_loop(0, fan, encode_back, 0)
    slot_half = slot_sum[...].astype(bf16)
    slot_back_out[...] = slot_half.reshape(slot_back_out.shape)
    slot_back_batch = exchange_grid(slot_back_out, slot_back_in)
    waiting["vec", 0] = [send(vec, vec_in.at[0], at_core(1))]
    receiver_low = receiver_sum[...].astype(bf16)
    put(0, 0, tn(slot_in[...].reshape(ng * cap, D), slot_half))
    put(0, 1, tn(latent, receiver_low))
    put(0, 2, tn(hidden0[...].reshape(fan * ng * cap, D), inner0[...].reshape(fan * ng * cap, D)))
    core_start(0)
    first_start(1)
    second_start(2)
    second_finish(3)
    mesh_grad[...] = lower_part + nt(receiver_low, w[1])
    store(mesh_grad, mesh_grad_hbm)
    first_start(0)

    def vec_step(batch_key, level, steps, start):
        arrive(waiting[batch_key])
        value = vec[...] if level == 0 else vec_sum[level - 1]
        for o in steps:
            value = value + vec_in[o]
        return value

    vec_sum[0] = vec_step(("vec", 0), 0, range(0, 1), 0)
    waiting["vec", 1] = [send(vec_sum.at[0], vec_in.at[o], at_y(o)) for o in range(1, ny)]
    second_finish(2)
    last_start(1)
    second_start(1)
    vec_sum[1] = vec_step(("vec", 1), 1, range(1, ny), 0)
    waiting["vec", 2] = [send(vec_sum.at[1], vec_in.at[ny - 1 + o], at_x(o)) for o in range(1, nx)]

    arrive(slot_back_batch)
    grid_half = mm(send_hot[...], slot_back_in[...].reshape(ng * cap, D)).astype(bf16)
    grid_grad[...] = nt(grid_half, w[0])
    store(grid_grad, grid_grad_hbm)

    second_start(0)
    vec_sum[2] = vec_step(("vec", 2), 2, range(ny, ny + nx - 1), 0)
    base = ny + nx - 2
    waiting["vec", 3] = [send(vec_sum.at[2], vec_in.at[base + o], at_z(o)) for o in range(1, nz)]
    second_finish(1)
    second_finish(0)
    last_start(0)
    upper = last_finish(1)
    vec_total = vec_step(("vec", 3), 3, range(base + 1, base + nz), 0) * scale
    lower = last_finish(0)
    pad = s["pad"]
    results = (lower[:pad], lower[pad:], upper[:pad], upper[pad:])
    first_device = flat == 0
    for j in range(4):
        shift_out[2 * j : 2 * j + 2, :] = jnp.where(first_device, vec_total[2 * j : 2 * j + 2], results[j][:2])
    shift = send(shift_out, shift_in, at_flat(-1))
    own = s["own"]
    for j in range(4):
        for r in range(own):
            shares[r, j : j + 1, :] = results[j][r : r + 1]
    arrive([shift])
    for j in range(4):
        for r in range(2):
            shares[own + r, j : j + 1, :] = shift_in[2 * j + r : 2 * j + r + 1, :]
    store(shares, shares_hbm)
    for copy in started:
        copy.wait_send()
    for copy in results_out:
        copy.wait()


def whole(s, scale, count, *refs):
    kernel(s, scale, refs[:count], *refs[count:])


def finish(s, total, upper, grid, lower, shares, upper_out, grid_out, lower_out, weight_out, *scratch):
    held, sem = scratch[:3], scratch[3]
    n = len(held)
    fetch = [
        pltpu.make_async_copy(source, target, sem.at[i])
        for i, (source, target) in enumerate(zip((upper, grid, lower), held))
    ]
    drain = [
        pltpu.make_async_copy(source, target, sem.at[n + i])
        for i, (source, target) in enumerate(zip(held, (upper_out, grid_out, lower_out)))
    ]
    for copy in fetch:
        copy.start()
    for here, there in zip(fetch, drain):
        here.wait()
        there.start()
    D = s["D"]
    joined = jnp.concatenate([shares[r] for r in range(s["out"])], axis=1)
    width = s["out"] * D
    extra = 2 * D // total
    start = (lax.axis_index("grid") * s["nm"] + lax.axis_index("mesh")) * extra
    rolled = pltpu.roll(joined, (width - start) % width, 1)
    weight_out[...] = rolled[:4, : s["own"] * D + extra]
    for copy in drain:
        copy.wait()


def local(grid_latent, mesh_latent, mesh_cotangent, weights, biases, norm_gains, send_rows, counts, targets,
          senders, receivers, halo_rows):
    G, D = grid_latent.shape
    M = mesh_latent.shape[0]
    fan, sources, cap = targets.shape[1:]
    E = senders.shape[1]
    s = sizes(G, M, D, E, cap, fan)
    ng, nm, ny, nx, nz = s["ng"], s["nm"], s["ny"], s["nx"], s["nz"]
    slots = ng * cap
    tiles = 2
    tile = E // tiles
    joined = M + nm * cap
    half = D // 2
    n = copies(s)
    scale = 1.0 / math.sqrt(M * ng * nm)
    vmem = pl.BlockSpec(memory_space=pltpu.VMEM)
    spread, mask, depth, perm, low_pad, high_pad = constants(s)
    operands = (
        send_rows, spread, mask, grid_latent, counts, depth, targets, halo_rows, senders, receivers,
        mesh_latent, biases, norm_gains, mesh_cotangent, perm, low_pad, high_pad,
    )
    named = (
        grid_latent, mesh_latent, mesh_cotangent, biases, norm_gains, send_rows, counts, targets, senders, receivers,
        halo_rows, spread, mask, depth, perm, low_pad, high_pad,
    )
    results = (
        jax.ShapeDtypeStruct((M, D), bf16), jax.ShapeDtypeStruct((G, D), f32),
        jax.ShapeDtypeStruct((M, D), f32), jax.ShapeDtypeStruct((s["out"], 8, D), f32),
    )
    scratch = [pltpu.VMEM(v.shape, v.dtype) for v in named + results] + [
        pltpu.VMEM(weights.shape, bf16),
        pltpu.VMEM((G, slots), bf16), pltpu.VMEM((fan, M, slots), bf16), pltpu.VMEM((M, nm * cap), bf16),
        pltpu.VMEM((tiles, joined + M, tile), bf16),
        pltpu.VMEM((ng, cap, D), bf16), pltpu.VMEM((ng, cap, D), bf16),
        pltpu.VMEM((nm, cap, D), bf16), pltpu.VMEM((nm, cap, D), bf16),
        pltpu.VMEM((nm, cap, D), bf16), pltpu.VMEM((nm, cap, D), bf16),
        pltpu.VMEM((ng, cap, D), bf16), pltpu.VMEM((ng, cap, D), bf16),
        pltpu.VMEM((slots, D), bf16),
        pltpu.VMEM((fan, slots, D), bf16), pltpu.VMEM((fan, slots, D), f32), pltpu.VMEM((fan, slots, D), f32),
        pltpu.VMEM((fan, slots, 1), f32), pltpu.VMEM((fan, slots, D), bf16),
        pltpu.VMEM((slots, D), f32), pltpu.VMEM((M, D), f32), pltpu.VMEM((M, D), f32),
        pltpu.VMEM((joined + M, D), bf16),
        pltpu.VMEM((tiles, tile, D), bf16), pltpu.VMEM((tiles, tile, D), f32), pltpu.VMEM((tiles, tile, D), f32),
        pltpu.VMEM((tiles, tile, 1), f32), pltpu.VMEM((tiles, tile, D), bf16), pltpu.VMEM((tiles, tile, D), bf16),
        pltpu.VMEM((4, 2, ny, s["zh"] * s["block"], D), bf16),
        pltpu.VMEM((4, ny, s["zh"] * s["block"], D), bf16),
        pltpu.VMEM((4, 2, nx, nx, s["plane"], half), bf16),
        pltpu.VMEM((4, 2, nx - 1, nx, s["plane"], half), bf16),
        pltpu.VMEM((4, 2, nx, s["plane"], half), bf16),
        pltpu.VMEM((4, 2, nx - 1, s["plane"], half), bf16),
        pltpu.VMEM((4, s["plane"], D), bf16),
        pltpu.VMEM((2, nz, 2 * s["pad"], D), bf16),
        pltpu.VMEM((2, nz - 1, 2 * s["pad"], D), bf16),
        pltpu.VMEM((8, D), f32), pltpu.VMEM((3, 8, D), f32), pltpu.VMEM((ny + nx + nz - 2, 8, D), f32),
        pltpu.VMEM((8, D), f32), pltpu.VMEM((8, D), f32),
        pltpu.SemaphoreType.DMA((weights.shape[0],)),
        pltpu.SemaphoreType.DMA((len(operands),)), pltpu.SemaphoreType.DMA((4,)),
        pltpu.SemaphoreType.DMA((n,)), pltpu.SemaphoreType.DMA((n,)),
    ]
    anywhere = pl.BlockSpec(memory_space=pl.ANY)
    mesh_out, grid_grad, mesh_grad, shares = pl.pallas_call(
        functools.partial(whole, s, scale, len(operands)),
        out_shape=results,
        in_specs=[anywhere] * (len(operands) + 1),
        out_specs=(anywhere,) * 4,
        scratch_shapes=scratch,
        compiler_params=pltpu.CompilerParams(
            collective_id=0, has_side_effects=True, vmem_limit_bytes=60 * 1024 * 1024
        ),
    )(*operands, weights)
    return tuple(
        pl.pallas_call(
            functools.partial(finish, s, ng * nm),
            out_shape=(
                jax.ShapeDtypeStruct((M, D), bf16), jax.ShapeDtypeStruct((G, D), f32),
                jax.ShapeDtypeStruct((M, D), f32),
                jax.ShapeDtypeStruct((4, s["own"] * D + 2 * D // (ng * nm)), f32),
            ),
            in_specs=[anywhere] * 3 + [vmem],
            out_specs=(anywhere, anywhere, anywhere, vmem),
            scratch_shapes=[pltpu.VMEM(v.shape, v.dtype) for v in results[:3]] + [pltpu.SemaphoreType.DMA((6,))],
            compiler_params=pltpu.CompilerParams(vmem_limit_bytes=60 * 1024 * 1024),
        )(mesh_out, grid_grad, mesh_grad, shares)
    )


def solution(mesh):
    both = ("grid", "mesh")
    placed = (
        P(both, None), P(both, None), P(both, None), P(), P(), P(), P(both, None, None), P(both, None),
        P(both, None, None, None), P(both, None), P(both, None), P(both, None, None),
    )
    return jax.shard_map(
        local, mesh=mesh, in_specs=placed,
        out_specs=(P(both, None), P(both, None), P(both, None), P(None, both)),
        check_vma=False,
    )
```

```python
import functools
import math

import jax
import jax.numpy as jnp
import numpy as np
from jax import lax
from jax.experimental import pallas as pl
from jax.experimental.pallas import tpu as pltpu
from jax.sharding import PartitionSpec as P

bf16 = jnp.bfloat16
f32 = jnp.float32
epsilon = 1e-05
MESH = pl.DeviceIdType.MESH
PARTS = (2, 4, 2, 4, 4)


def mm(left, right):
    return jnp.dot(left, right, preferred_element_type=f32)


def tn(left, right):
    return lax.dot_general(left, right, (((0,), (0,)), ((), ())), preferred_element_type=f32)


def nt(left, right):
    return lax.dot_general(left, right, (((1,), (1,)), ((), ())), preferred_element_type=f32)


def row_mean(values):
    return jnp.mean(values, axis=-1, keepdims=True)


def column_sum(values):
    return jnp.sum(values, axis=0, keepdims=True)


def forward(x, out_weight):
    sigmoid = 0.5 * jnp.tanh(0.5 * x) + 0.5
    active = x * sigmoid
    slope = active * (1.0 - sigmoid) + sigmoid
    hidden = active.astype(bf16)
    projected = mm(hidden, out_weight)
    centered = projected - row_mean(projected)
    reciprocal = lax.rsqrt(row_mean(centered * centered) + epsilon)
    return hidden, slope, centered * reciprocal, reciprocal


def backward(upstream, gain, normed, reciprocal, slope, out_weight):
    gain_grad = column_sum(upstream * normed)
    weighted = upstream * gain
    inner = reciprocal * (weighted - row_mean(weighted) - normed * row_mean(weighted * normed))
    inner = inner.astype(bf16)
    summed_grad = nt(inner, out_weight) * slope
    return summed_grad.astype(bf16), inner, column_sum(summed_grad), gain_grad


def sizes(grid_dev, mesh_dev, features, edges, cap, fan):
    zh, ny, nc, zl, nx = PARTS
    own = 3 * features // (zh * ny * nc * zl * nx)
    pad = -(-own // 8) * 8
    return dict(
        G=grid_dev, M=mesh_dev, D=features, E=edges, cap=cap, fan=fan, zh=zh, ny=ny, nc=nc, zl=zl, nx=nx,
        nz=zh * zl, ng=zh * ny * nc, nm=zl * nx, own=own, pad=pad, out=-(-(own + 2) // 8) * 8,
        block=3 * features // (zh * ny * nc), plane=zh * zl * own,
    )


def constants(s):
    slots = s["ng"] * s["cap"]
    at = np.arange(slots)
    spread = (at[None, :] % s["cap"] == np.arange(s["cap"])[:, None]).astype(np.float32)
    mask = (at[None, :] // s["cap"] == np.arange(s["ng"])[:, None]).astype(np.float32)
    depth = (at % s["cap"]).astype(np.float32)[None, :]
    rows = s["nx"] * s["nz"] * s["own"]
    perm = np.zeros((rows, rows), np.float32)
    low = np.zeros((s["nz"] * 2 * s["pad"], s["plane"]), np.float32)
    high = np.zeros_like(low)
    for z in range(s["nz"]):
        for i in range(s["own"]):
            for x in range(s["nx"]):
                perm[x * s["plane"] + z * s["own"] + i, (z * s["nx"] + x) * s["own"] + i] = 1
            low[z * 2 * s["pad"] + i, z * s["own"] + i] = 1
            high[z * 2 * s["pad"] + s["pad"] + i, z * s["own"] + i] = 1
    return (
        jnp.asarray(spread, f32), jnp.asarray(mask, f32), jnp.asarray(depth, f32),
        jnp.asarray(perm, f32), jnp.asarray(low, f32), jnp.asarray(high, f32),
    )


def copies(s):
    kinds = dict(
        a2a=2 * (s["ng"] - 1) + 2 * (s["nm"] - 1), core=4, first=4 * (s["ny"] + s["nx"] - 2),
        second=4 * (s["ny"] + s["nx"] - 2), last=2 * (s["nz"] - 1),
        vec=1 + s["ny"] - 1 + s["nx"] - 1 + s["nz"] - 1, shift=1,
    )
    return sum(kinds.values())


def kernel(
    s, scale,
    sources, weights, mesh_out_hbm, grid_grad_hbm, mesh_grad_hbm, shares_hbm,
    grid_latent, mesh_latent, cotangent, biases, gains, send_rows, counts, targets, senders, receivers,
    halo_rows, spread, mask, depth, perm, low_pad, high_pad,
    mesh_out, grid_grad, mesh_grad, shares,
    w, send_hot, target_hot, halo_hot, edge_hot,
    slot_out, slot_in, halo_out, halo_in, back_out, back_in, slot_back_out, slot_back_in,
    hidden0, slope0, normed0, recip0, inner0, gather_sum,
    table, hidden2, slope2, normed2, recip2, inner2, grad2,
    bucket, core_in, split, first_in, partial, second_in, plane, last_out, last_in,
    vec, vec_sum, vec_in, shift_out, shift_in,
    weight_sem, input_sem, output_sem, send_sem, recv_sem,
):
    D, M, cap, fan = s["D"], s["M"], s["cap"], s["fan"]
    zh, ny, nc, zl, nx, nz, ng, nm = (s[k] for k in ("zh", "ny", "nc", "zl", "nx", "nz", "ng", "nm"))
    gi, mi = lax.axis_index("grid"), lax.axis_index("mesh")
    core = gi % nc
    y = (gi // nc) % ny
    z_hi = gi // (nc * ny)
    x = mi % nx
    z_lo = mi // nx
    z = z_hi * zl + z_lo
    flat = gi * nm + mi
    total = ng * nm

    def at_core(o):
        return ((z_hi * ny + y) * nc + (core + o) % nc, mi)

    def at_y(o):
        return ((z_hi * ny + (y + o) % ny) * nc + core, mi)

    def at_x(o):
        return (gi, z_lo * nx + (x + o) % nx)

    def at_z(o):
        to = (z + o) % nz
        return (((to // zl) * ny + y) * nc + core, (to % zl) * nx + x)

    def at_flat(o):
        to = (flat + o + total) % total
        return (to // nm, to % nm)

    operands = (
        send_rows, spread, mask, grid_latent, counts, depth, targets, halo_rows, senders, receivers,
        mesh_latent, biases, gains, cotangent, perm, low_pad, high_pad,
    )
    fetch = [pltpu.make_async_copy(a, b, input_sem.at[i]) for i, (a, b) in enumerate(zip(sources, operands))]
    for copy in fetch[:4]:
        copy.start()
    results_out = []

    def store(value_ref, target):
        copy = pltpu.make_async_copy(value_ref, target, output_sem.at[len(results_out)])
        copy.start()
        results_out.append(copy)

    order = (1, 3, 0, 2, 4, 5, 6, 7, 9, 8, 10, 11)
    loads = {i: pltpu.make_async_copy(weights.at[i], w.at[i], weight_sem.at[i]) for i in order}

    barrier = pltpu.get_barrier_semaphore()
    greeted = [((gi + o) % ng, mi) for o in range(1, ng)] + [(gi, (mi + o) % nm) for o in range(1, nm)]
    for a in range(1, zh):
        for b in range(1, zl):
            greeted.append(
                ((((z_hi + a) % zh) * ny + y) * nc + core, ((z_lo + b) % zl) * nx + x)
            )
    greeted += [at_flat(1), at_flat(-1)]
    for device in greeted:
        pl.semaphore_signal(barrier, inc=1, device_id=device, device_id_type=MESH)

    ids = iter(range(copies(s)))
    started = []

    def send(source, target, device):
        i = next(ids)
        copy = pltpu.make_async_remote_copy(
            src_ref=source, dst_ref=target, send_sem=send_sem.at[i], recv_sem=recv_sem.at[i],
            device_id=device, device_id_type=MESH,
        )
        copy.start()
        started.append(copy)
        return copy

    def far_first(n):
        return sorted(range(1, n), key=lambda o: -min(o, n - o))

    def arrive(batch):
        for copy in batch:
            copy.wait_recv()

    ring = ny * nc
    lane = gi % ring

    def exchange_grid(out, into, dz):
        batch = []
        for o in range(1 if dz == 0 else 0, ring):
            to = ((z_hi + dz) % zh) * ring + (lane + o) % ring
            batch.append(send(out.at[to], into.at[gi], (to, mi)))
        if dz == 0:
            into[pl.ds(gi, 1)] = out[pl.ds(gi, 1)]
        return batch

    def exchange_mesh(out, into):
        batch = []
        for dz in sorted(range(zl), key=lambda d: -min(d, zl - d)):
            for o in range(1 if dz == 0 else 0, nx):
                to = ((z_lo + dz) % zl) * nx + (x + o) % nx
                batch.append(send(out.at[to], into.at[mi], (gi, to)))
        into[pl.ds(mi, 1)] = out[pl.ds(mi, 1)]
        return batch

    def lay(values):
        spread_out = mm(values.astype(f32).astype(bf16), spread[...].astype(bf16))
        return column_sum(spread_out * mask[...])

    def one_hot(rows, nodes):
        node = lax.broadcasted_iota(jnp.int32, (nodes, rows.shape[1]), 0).astype(f32)
        return jnp.where(node == rows, 1.0, 0.0).astype(bf16)

    for copy in fetch[:4]:
        copy.wait()
    send_hot[...] = one_hot(lay(send_rows[0]), s["G"])
    slot_out[...] = tn(send_hot[...], grid_latent[...]).astype(bf16).reshape(slot_out.shape)
    pl.semaphore_wait(barrier, len(greeted))
    slots_batch = [None] * zh
    for dz in reversed(range(zh)):
        slots_batch[dz] = exchange_grid(slot_out, slot_in, dz)

    for copy in fetch[4:11]:
        copy.start()
    for i in order[:4]:
        loads[i].start()
    for copy in fetch[11:]:
        copy.start()
    for i in order[4:]:
        loads[i].start()
    for copy in fetch[4:]:
        copy.wait()
    count_row = mm(counts[...].astype(f32).astype(bf16), mask[...].astype(bf16))
    live = depth[...] < count_row
    part = ring * cap
    for k in range(fan):
        target_row = jnp.where(live, lay(targets[0, k]), -1.0)
        for a in range(zh):
            target_hot[a, :, k * part : (k + 1) * part] = one_hot(target_row[:, a * part : (a + 1) * part], M)
    halo_hot[...] = one_hot(lay(halo_rows[0]), M)
    tiles, _, tile = edge_hot.shape
    joined = M + nm * cap
    for t in range(tiles):
        piece = pl.ds(t * tile, tile)
        edge_hot[t, :joined] = one_hot(senders[:, piece].astype(f32), joined)
        edge_hot[t, joined:] = one_hot(receivers[:, piece].astype(f32), M)

    loads[1].wait()
    latent = mesh_latent[...]
    receiver_terms = mm(latent, w[1]).astype(bf16)
    loads[3].wait()
    low_part = mm(latent, w[3])
    loads[0].wait()
    loads[2].wait()

    gathered = None
    for t in range(zh):
        away = (z_hi + t) % zh
        arrive(slots_batch[t])
        here = pl.ds(away * ring, ring)
        terms = mm(slot_in[here].reshape(part, D), w[0]).astype(bf16).astype(f32)
        hot = target_hot[away]
        x0 = jnp.concatenate([terms] * fan, axis=0) + tn(hot, receiver_terms) + biases[0:1, :]
        hidden, slope, normed, recip = forward(x0, w[2])
        hidden0[t] = hidden
        slope0[t] = slope
        normed0[t] = normed
        recip0[t] = recip
        message = mm(hot, (normed * gains[0:1, :]).astype(bf16))
        gathered = message if gathered is None else gathered + message
    grid_gathered = gathered.astype(bf16)

    loads[4].wait()
    loads[5].wait()
    x1 = low_part + mm(grid_gathered, w[4]) + biases[1:2, :]
    hidden1, slope1, normed1, recip1 = forward(x1, w[5])
    middle = (latent.astype(f32) + normed1 * gains[1:2, :]).astype(bf16)
    halo_out[...] = tn(halo_hot[...], middle).astype(bf16).reshape(halo_out.shape)
    halo_batch = exchange_mesh(halo_out, halo_in)

    for i in (6, 7, 9, 8):
        loads[i].wait()
    table[:M] = mm(middle, w[6]).astype(bf16)
    table[joined:] = mm(middle, w[7]).astype(bf16)
    top_part = mm(middle, w[9]) + biases[3:4, :]

    arrive(halo_batch)
    halo_rows_in = halo_in[...].reshape(nm * cap, D)
    table[M:joined] = mm(halo_rows_in, w[6]).astype(bf16)
    gather_sum[...] = jnp.zeros_like(gather_sum)

    def process(t, carry):
        x2 = tn(edge_hot[t], table[...]) + biases[2:3, :]
        hidden, slope, normed, recip = forward(x2, w[8])
        hidden2[t] = hidden
        slope2[t] = slope
        normed2[t] = normed
        recip2[t] = recip
        gather_sum[...] += mm(edge_hot[t, joined:], (normed * gains[2:3, :]).astype(bf16))
        return carry

    lax.fori_loop(0, tiles, process, 0)
    mesh_gathered = gather_sum[...].astype(bf16)

    loads[10].wait()
    loads[11].wait()
    x3 = top_part + mm(mesh_gathered, w[10])
    hidden3, slope3, normed3, recip3 = forward(x3, w[11])
    mesh_out[...] = (middle.astype(f32) + normed3 * gains[3:4, :]).astype(bf16)
    store(mesh_out, mesh_out_hbm)
    upstream = cotangent[...].astype(f32)
    grad3, inner3, bias_grad, gain_grad = backward(upstream, gains[3:4, :], normed3, recip3, slope3, w[11])
    vec[6:7, :] = bias_grad
    vec[7:8, :] = gain_grad
    gathered_grad = nt(grad3, w[10]).astype(bf16)
    middle_part = upstream + nt(grad3, w[9])

    def put(j, m, value):
        value = value.astype(bf16)
        for r in range(0, D, 32):
            a, rest = divmod(m * D + r, ny * nc * s["block"])
            b, rest = divmod(rest, nc * s["block"])
            c, q = divmod(rest, s["block"])
            bucket[j, c, b, a * s["block"] + q : a * s["block"] + q + 32, :] = value[r : r + 32]

    half = D // 2
    rows = s["plane"]
    waiting = {}

    def core_start(j):
        waiting["core", j] = [send(bucket.at[j, 1 - core], core_in.at[j], at_core(1))]

    def first_start(j):
        arrive(waiting["core", j])

        def fold(b, carry):
            both = bucket[j, core, b].astype(f32) + core_in[j, b].astype(f32)
            moved = mm(perm[...].astype(bf16), both.astype(bf16)).astype(bf16)
            for a in range(nx):
                split[j, 0, b, a] = moved[a * rows : (a + 1) * rows, :half]
                split[j, 1, a, b] = moved[a * rows : (a + 1) * rows, half:]
            return carry

        lax.fori_loop(0, ny, fold, 0)
        waiting["first", j] = [
            send(split.at[j, 0, (y + o) % ny], first_in.at[j, 0, o - 1], at_y(o)) for o in far_first(ny)
        ]

    def first_other(j):
        waiting["first", j] += [
            send(split.at[j, 1, (x + o) % nx], first_in.at[j, 1, o - 1], at_x(o)) for o in far_first(nx)
        ]

    def second_start(j):
        arrive(waiting["first", j])
        for h, mine, n in ((0, y, ny), (1, x, nx)):
            value = split[j, h, mine].astype(f32)
            for o in range(n - 1):
                value = value + first_in[j, h, o].astype(f32)
            partial[j, h] = value.astype(bf16)
        waiting["second", j] = [
            send(partial.at[j, 0, (x + o) % nx], second_in.at[j, 0, o - 1], at_x(o)) for o in far_first(nx)
        ] + [send(partial.at[j, 1, (y + o) % ny], second_in.at[j, 1, o - 1], at_y(o)) for o in far_first(ny)]

    def second_finish(j):
        arrive(waiting["second", j])
        for h, mine, n in ((0, x, nx), (1, y, ny)):
            value = partial[j, h, mine].astype(f32)
            for o in range(n - 1):
                value = value + second_in[j, h, o].astype(f32)
            plane[j, :, h * half : (h + 1) * half] = value.astype(bf16)

    def last_start(p):
        padded = mm(low_pad[...].astype(bf16), plane[2 * p]) + mm(high_pad[...].astype(bf16), plane[2 * p + 1])
        last_out[p] = padded.astype(bf16).reshape(last_out.shape[1:])
        waiting["last", p] = [
            send(last_out.at[p, (z + o) % nz], last_in.at[p, o - 1], at_z(o)) for o in far_first(nz)
        ]

    def last_finish(p):
        arrive(waiting["last", p])
        value = last_out[p, z].astype(f32)
        for o in range(nz - 1):
            value = value + last_in[p, o].astype(f32)
        return value * scale

    put(3, 0, tn(middle, grad3))
    put(3, 1, tn(mesh_gathered, grad3))
    put(3, 2, tn(hidden3, inner3))
    core_start(3)

    vec[4:6, :] = jnp.zeros((2, D), f32)

    def process_back(t, carry):
        up = tn(edge_hot[t, joined:], gathered_grad)
        grad, inner, bias_part, gain_part = backward(up, gains[2:3, :], normed2[t], recip2[t], slope2[t], w[8])
        inner2[t] = inner
        grad2[t] = grad
        vec[4:5, :] += bias_part
        vec[5:6, :] += gain_part
        return carry

    lax.fori_loop(0, tiles, process_back, 0)
    spread_grad = mm(edge_hot[0], grad2[0])
    for t in range(1, tiles):
        spread_grad = spread_grad + mm(edge_hot[t], grad2[t])
    spread_half = spread_grad.astype(bf16)
    back_out[...] = spread_half[M:joined].reshape(back_out.shape)
    back_batch = exchange_mesh(back_out, back_in)
    receiver_half = spread_half[joined:]
    first_start(3)
    put(2, 0, tn(middle, spread_half[:M]) + tn(halo_rows_in, spread_half[M:joined]))
    put(2, 1, tn(middle, receiver_half))
    put(2, 2, tn(hidden2[...].reshape(tiles * tile, D), inner2[...].reshape(tiles * tile, D)))
    core_start(2)
    middle_part = middle_part + nt(receiver_half, w[7])
    first_start(2)
    arrive(back_batch)
    first_other(3)
    first_other(2)
    returned = mm(halo_hot[...], back_in[...].reshape(nm * cap, D))
    sender_half = (spread_grad[:M] + returned).astype(bf16)
    middle_grad = middle_part + nt(sender_half, w[6])

    grad1, inner1, bias_grad, gain_grad = backward(middle_grad, gains[1:2, :], normed1, recip1, slope1, w[5])
    vec[2:3, :] = bias_grad
    vec[3:4, :] = gain_grad
    low_gathered_grad = nt(grad1, w[4]).astype(bf16)

    slot_back_batch = []
    receiver_low = None
    totals = []
    for t in reversed(range(zh)):
        away = (z_hi + t) % zh
        hot = target_hot[away]
        up = tn(hot, low_gathered_grad)
        grad, inner, bias_part, gain_part = backward(up, gains[0:1, :], normed0[t], recip0[t], slope0[t], w[2])
        inner0[t] = inner
        slot_grad = grad[:part].astype(f32)
        for k in range(1, fan):
            slot_grad = slot_grad + grad[k * part : (k + 1) * part].astype(f32)
        slot_back_out[pl.ds(away * ring, ring)] = slot_grad.astype(bf16).reshape(ring, cap, D)
        slot_back_batch += exchange_grid(slot_back_out, slot_back_in, t)
        low = mm(hot, grad)
        receiver_low = low if receiver_low is None else receiver_low + low
        totals.append((bias_part, gain_part))
        if t == zh - 1:
            put(1, 0, tn(latent, grad1))
            put(1, 1, tn(grid_gathered, grad1))
            put(1, 2, tn(hidden1, inner1))
            core_start(1)
    vec[0:1, :] = sum(a for a, _ in totals[1:]) + totals[0][0]
    vec[1:2, :] = sum(b for _, b in totals[1:]) + totals[0][1]
    waiting["vec", 0] = [send(vec, vec_in.at[0], at_core(1))]
    receiver_low = receiver_low.astype(bf16)
    put(0, 2, tn(hidden0[...].reshape(fan * ng * cap, D), inner0[...].reshape(fan * ng * cap, D)))
    put(0, 0, tn(slot_in[...].reshape(ng * cap, D), slot_back_out[...].reshape(ng * cap, D)))
    put(0, 1, tn(latent, receiver_low))
    core_start(0)
    first_start(1)
    first_other(1)
    first_start(0)
    first_other(0)

    def vec_step(level, steps):
        arrive(waiting["vec", level])
        value = vec[...] if level == 0 else vec_sum[level - 1]
        for o in steps:
            value = value + vec_in[o]
        return value

    second_start(3)
    second_start(2)
    vec_sum[0] = vec_step(0, range(0, 1))
    waiting["vec", 1] = [send(vec_sum.at[0], vec_in.at[o], at_y(o)) for o in range(1, ny)]
    mesh_grad[...] = middle_grad + nt(grad1, w[3]) + nt(receiver_low, w[1])
    store(mesh_grad, mesh_grad_hbm)
    second_finish(3)
    second_finish(2)
    last_start(1)
    vec_sum[1] = vec_step(1, range(1, ny))
    waiting["vec", 2] = [send(vec_sum.at[1], vec_in.at[ny - 1 + o], at_x(o)) for o in range(1, nx)]

    arrive(slot_back_batch)
    grid_half = mm(send_hot[...], slot_back_in[...].reshape(ng * cap, D)).astype(bf16)
    grid_grad[...] = nt(grid_half, w[0])
    store(grid_grad, grid_grad_hbm)

    second_start(1)
    vec_sum[2] = vec_step(2, range(ny, ny + nx - 1))
    base = ny + nx - 2
    waiting["vec", 3] = [send(vec_sum.at[2], vec_in.at[base + o], at_z(o)) for o in range(1, nz)]
    second_start(0)
    second_finish(1)
    second_finish(0)
    sent = len(started)
    last_start(0)
    upper = last_finish(1)
    for copy in started[:sent]:
        copy.wait_send()
    vec_total = vec_step(3, range(base + 1, base + nz)) * scale
    lower = last_finish(0)
    pad = s["pad"]
    results = (lower[:pad], lower[pad:], upper[:pad], upper[pad:])
    first_device = flat == 0
    for j in range(4):
        shift_out[2 * j : 2 * j + 2, :] = jnp.where(first_device, vec_total[2 * j : 2 * j + 2], results[j][:2])
    shift = send(shift_out, shift_in, at_flat(-1))
    own = s["own"]
    for j in range(4):
        for r in range(own):
            shares[r, j : j + 1, :] = results[j][r : r + 1]
    arrive([shift])
    for j in range(4):
        for r in range(2):
            shares[own + r, j : j + 1, :] = shift_in[2 * j + r : 2 * j + r + 1, :]
    store(shares, shares_hbm)
    for copy in started[sent:]:
        copy.wait_send()
    for copy in results_out:
        copy.wait()


def whole(s, scale, count, *refs):
    kernel(s, scale, refs[:count], *refs[count:])


def finish(s, total, *refs):
    sources, targets, held, turned, sem = refs[:4], refs[4:8], refs[8:12], refs[12], refs[13]
    fetch = [pltpu.make_async_copy(a, b, sem.at[i]) for i, (a, b) in enumerate(zip(sources, held))]
    ready = tuple(held[:3]) + (turned,)
    drain = [pltpu.make_async_copy(a, b, sem.at[4 + i]) for i, (a, b) in enumerate(zip(ready, targets))]
    for i in (3, 1, 2, 0):
        fetch[i].start()
    fetch[3].wait()
    D = s["D"]
    joined = jnp.concatenate([held[3][r] for r in range(s["out"])], axis=1)
    width = s["out"] * D
    extra = 2 * D // total
    start = (lax.axis_index("grid") * s["nm"] + lax.axis_index("mesh")) * extra
    rolled = pltpu.roll(joined, (width - start) % width, 1)
    for i in (1, 2, 0):
        fetch[i].wait()
        drain[i].start()
    turned[...] = rolled[:4, : s["own"] * D + extra]
    drain[3].start()
    for copy in drain:
        copy.wait()


def local(grid_latent, mesh_latent, mesh_cotangent, weights, biases, norm_gains, send_rows, counts, targets,
          senders, receivers, halo_rows):
    G, D = grid_latent.shape
    M = mesh_latent.shape[0]
    fan, sources, cap = targets.shape[1:]
    E = senders.shape[1]
    s = sizes(G, M, D, E, cap, fan)
    ng, nm, ny, nx, nz = s["ng"], s["nm"], s["ny"], s["nx"], s["nz"]
    slots = ng * cap
    wide = fan * slots // s["zh"]
    tiles = 2
    tile = E // tiles
    joined = M + nm * cap
    half = D // 2
    n = copies(s)
    scale = 1.0 / math.sqrt(M * ng * nm)
    vmem = pl.BlockSpec(memory_space=pltpu.VMEM)
    spread, mask, depth, perm, low_pad, high_pad = constants(s)
    operands = (
        send_rows, spread, mask, grid_latent, counts, depth, targets, halo_rows, senders, receivers,
        mesh_latent, biases, norm_gains, mesh_cotangent, perm, low_pad, high_pad,
    )
    named = (
        grid_latent, mesh_latent, mesh_cotangent, biases, norm_gains, send_rows, counts, targets, senders, receivers,
        halo_rows, spread, mask, depth, perm, low_pad, high_pad,
    )
    results = (
        jax.ShapeDtypeStruct((M, D), bf16), jax.ShapeDtypeStruct((G, D), f32),
        jax.ShapeDtypeStruct((M, D), f32), jax.ShapeDtypeStruct((s["out"], 8, D), f32),
    )
    scratch = [pltpu.VMEM(v.shape, v.dtype) for v in named + results] + [
        pltpu.VMEM(weights.shape, bf16),
        pltpu.VMEM((G, slots), bf16), pltpu.VMEM((s["zh"], M, wide), bf16), pltpu.VMEM((M, nm * cap), bf16),
        pltpu.VMEM((tiles, joined + M, tile), bf16),
        pltpu.VMEM((ng, cap, D), bf16), pltpu.VMEM((ng, cap, D), bf16),
        pltpu.VMEM((nm, cap, D), bf16), pltpu.VMEM((nm, cap, D), bf16),
        pltpu.VMEM((nm, cap, D), bf16), pltpu.VMEM((nm, cap, D), bf16),
        pltpu.VMEM((ng, cap, D), bf16), pltpu.VMEM((ng, cap, D), bf16),
        pltpu.VMEM((s["zh"], wide, D), bf16), pltpu.VMEM((s["zh"], wide, D), f32),
        pltpu.VMEM((s["zh"], wide, D), f32), pltpu.VMEM((s["zh"], wide, 1), f32),
        pltpu.VMEM((s["zh"], wide, D), bf16), pltpu.VMEM((M, D), f32),
        pltpu.VMEM((joined + M, D), bf16),
        pltpu.VMEM((tiles, tile, D), bf16), pltpu.VMEM((tiles, tile, D), f32), pltpu.VMEM((tiles, tile, D), f32),
        pltpu.VMEM((tiles, tile, 1), f32), pltpu.VMEM((tiles, tile, D), bf16), pltpu.VMEM((tiles, tile, D), bf16),
        pltpu.VMEM((4, 2, ny, s["zh"] * s["block"], D), bf16),
        pltpu.VMEM((4, ny, s["zh"] * s["block"], D), bf16),
        pltpu.VMEM((4, 2, nx, nx, s["plane"], half), bf16),
        pltpu.VMEM((4, 2, nx - 1, nx, s["plane"], half), bf16),
        pltpu.VMEM((4, 2, nx, s["plane"], half), bf16),
        pltpu.VMEM((4, 2, nx - 1, s["plane"], half), bf16),
        pltpu.VMEM((4, s["plane"], D), bf16),
        pltpu.VMEM((2, nz, 2 * s["pad"], D), bf16),
        pltpu.VMEM((2, nz - 1, 2 * s["pad"], D), bf16),
        pltpu.VMEM((8, D), f32), pltpu.VMEM((3, 8, D), f32), pltpu.VMEM((ny + nx + nz - 2, 8, D), f32),
        pltpu.VMEM((8, D), f32), pltpu.VMEM((8, D), f32),
        pltpu.SemaphoreType.DMA((weights.shape[0],)),
        pltpu.SemaphoreType.DMA((len(operands),)), pltpu.SemaphoreType.DMA((4,)),
        pltpu.SemaphoreType.DMA((n,)), pltpu.SemaphoreType.DMA((n,)),
    ]
    anywhere = pl.BlockSpec(memory_space=pl.ANY)
    mesh_out, grid_grad, mesh_grad, shares = pl.pallas_call(
        functools.partial(whole, s, scale, len(operands)),
        out_shape=results,
        in_specs=[anywhere] * (len(operands) + 1),
        out_specs=(anywhere,) * 4,
        scratch_shapes=scratch,
        compiler_params=pltpu.CompilerParams(
            collective_id=0, has_side_effects=True, vmem_limit_bytes=60 * 1024 * 1024
        ),
    )(*operands, weights)
    return tuple(
        pl.pallas_call(
            functools.partial(finish, s, ng * nm),
            out_shape=(
                jax.ShapeDtypeStruct((M, D), bf16), jax.ShapeDtypeStruct((G, D), f32),
                jax.ShapeDtypeStruct((M, D), f32),
                jax.ShapeDtypeStruct((4, s["own"] * D + 2 * D // (ng * nm)), f32),
            ),
            in_specs=[anywhere] * 4,
            out_specs=(anywhere,) * 4,
            scratch_shapes=[pltpu.VMEM(v.shape, v.dtype) for v in results]
            + [pltpu.VMEM((4, s["own"] * D + 2 * D // (ng * nm)), f32), pltpu.SemaphoreType.DMA((8,))],
            compiler_params=pltpu.CompilerParams(vmem_limit_bytes=60 * 1024 * 1024),
        )(mesh_out, grid_grad, mesh_grad, shares)
    )


def solution(mesh):
    both = ("grid", "mesh")
    placed = (
        P(both, None), P(both, None), P(both, None), P(), P(), P(), P(both, None, None), P(both, None),
        P(both, None, None, None), P(both, None), P(both, None), P(both, None, None),
    )
    return jax.shard_map(
        local, mesh=mesh, in_specs=placed,
        out_specs=(P(both, None), P(both, None), P(both, None), P(None, both)),
        check_vma=False,
    )
```
